32 devices in a mesh: ctx: 8 (over z, core), tp: 4 (over y, x).
Axes of the slice: x: 2, y: 2, z: 4, core: 2. Of those that a mesh axis runs over, the one named last changes fastest.
Arguments:
- x_in: bfloat16 [1024, 16384], P('ctx', 'tp'), may hold values from -6 to 6
- z_in: bfloat16 [1024, 16384], P('ctx', 'tp'), may hold values from -6 to 6
- b_in: bfloat16 [1024, 512], P('ctx', 'tp'), may hold values from -6 to 6
- c_in: bfloat16 [1024, 512], P('ctx', 'tp'), may hold values from -6 to 6
- dt_raw: float32 [1024, 256], P('ctx', 'tp'), may hold values from -2 to 2
- dt_bias: float32 [256], P('tp'), may hold values from -5.8 to -4.2
- a_log: float32 [256], P('tp'), may hold values from -2 to 1.1
- d_skip: float32 [256], P('tp'), may hold values from 0.5 to 1.5
- conv_x: float32 [4, 16384], P(None, 'tp'), may hold values from -3 to 3
- conv_b: float32 [4, 512], P(None, 'tp'), may hold values from -3 to 3
- conv_c: float32 [4, 512], P(None, 'tp'), may hold values from -3 to 3
- norm_gain: float32 [16384], P('tp'), may hold values from 0.1 to 1.9
Outputs:
- mixed_out: bfloat16 [16384, 1024], P(('tp', 'ctx'))
The draws below stay inside these ranges and needn't reach their ends.
All inputs are finite; a program needn't handle non-finite values.
Results may differ from the reference program's by a relative error of at most 0.007.
Values may be sent and summed in bfloat16 or wider, within the bound.
A program may use at most 128 MiB of HBM per device.

```python
import jax
import jax.numpy as jnp
from jax import lax

HEADS = 256
HEAD_DIM = 64
STATE = 128
CONV = 4
SPAN = 128
TOK_DEV = 128
TOKENS = 1024
GROUPS = 4
HEADS_DEV = 64
CHANNELS = 16384


def head_kinds(key):
    share = 0.5
    return jax.random.uniform(jax.random.fold_in(key, 11), (HEADS,)) < share


def draw_a_log(key, part):
    slower = head_kinds(key)
    slow_values = jax.random.uniform(jax.random.fold_in(key, 12), (HEADS,), jnp.float32, -1.8, -0.4)
    fast_values = jax.random.uniform(jax.random.fold_in(key, 13), (HEADS,), jnp.float32, 0.3, 1.1)
    return jnp.where(slower, slow_values, fast_values)


def draw_dt_bias(key, part):
    slower = head_kinds(key)
    slow_values = jax.random.uniform(jax.random.fold_in(key, 14), (HEADS,), jnp.float32, -5.8, -5.2)
    fast_values = jax.random.uniform(jax.random.fold_in(key, 15), (HEADS,), jnp.float32, -4.6, -4.2)
    return jnp.where(slower, slow_values, fast_values)


def draw_dt_raw(key, part):
    offsets = jax.random.uniform(jax.random.fold_in(key, 21), (TOKENS // TOK_DEV, 1, HEADS), jnp.float32, -0.7, 0.7)
    noise = 0.5 * jnp.clip(jax.random.normal(jax.random.fold_in(key, 23), (TOKENS // TOK_DEV, TOK_DEV, HEADS), jnp.float32), -2.5, 2.5)
    return (offsets + noise).reshape(TOKENS, HEADS)


def level_of(key, dims, cuts, low, high):
    loudness = 1.0
    for position, parts in cuts:
        steps = jax.random.uniform(jax.random.fold_in(jax.random.fold_in(key, 6), position), (parts,), jnp.float32, low / len(cuts), high / len(cuts))
        loudness = loudness * jnp.repeat(jnp.exp(steps), dims[position] // parts).reshape((-1,) + (1,) * (len(dims) - 1 - position))
    return loudness


def gaussian(rng, extent, scale, bound, split=(), held_as=jnp.bfloat16):
    result = scale * jax.random.normal(rng, extent, jnp.float32)
    if split:
        result = result * level_of(rng, extent, split, -0.22, 0.18)
    return jnp.clip(result, -bound, bound).astype(held_as)


def setup_inputs(seed: int = 0) -> dict:
    splits = jax.random.split(jax.random.key(seed), 13)
    x_in = gaussian(splits[0], (TOKENS, CHANNELS), 1.0, 6.0, ((0, 8), (1, 4)))
    z_in = gaussian(splits[1], (TOKENS, CHANNELS), 1.0, 6.0, ((0, 8), (1, 4)))
    b_in = gaussian(splits[2], (TOKENS, GROUPS * STATE), 1.0, 6.0, ((0, 8), (1, 4)))
    c_in = gaussian(splits[3], (TOKENS, GROUPS * STATE), 1.0, 6.0, ((0, 8), (1, 4)))
    dt_raw = draw_dt_raw(jax.random.fold_in(splits[12], 71), 0)
    dt_bias = draw_dt_bias(jax.random.fold_in(splits[12], 71), 0)
    a_log = draw_a_log(jax.random.fold_in(splits[12], 71), 0)
    d_skip = jnp.clip(0.5 + 1.0 * jax.random.uniform(splits[7], (HEADS,), jnp.float32) ** level_of(splits[7], (HEADS,), ((0, 4),), -0.2, 0.2), 0.5, 1.5)
    conv_x = gaussian(splits[8], (CONV, CHANNELS), CONV ** -0.5, 3.0, ((1, 4),), jnp.float32)
    conv_b = gaussian(splits[9], (CONV, GROUPS * STATE), CONV ** -0.5, 3.0, ((1, 4),), jnp.float32)
    conv_c = gaussian(splits[10], (CONV, GROUPS * STATE), CONV ** -0.5, 3.0, ((1, 4),), jnp.float32)
    norm_gain = jnp.clip(1.0 + 0.18 * jax.random.normal(splits[11], (CHANNELS,), jnp.float32), 0.1, 1.9)
    return dict(x_in=x_in, z_in=z_in, b_in=b_in, c_in=c_in, dt_raw=dt_raw, dt_bias=dt_bias, a_log=a_log, d_skip=d_skip, conv_x=conv_x, conv_b=conv_b, conv_c=conv_c, norm_gain=norm_gain)


def causal_silu(padded, taps):
    rows_f = padded.astype(jnp.float32)
    total = taps[0] * rows_f[0:SPAN]
    for offset in range(1, CONV):
        total = total + taps[offset] * rows_f[offset:offset + SPAN]
    return jax.nn.silu(total).astype(jnp.bfloat16)

def rounded(value):
    return lax.optimization_barrier(value.astype(jnp.bfloat16)).astype(jnp.float32)

def reference(x_in, z_in, b_in, c_in, dt_raw, dt_bias, a_log, d_skip, conv_x, conv_b, conv_c, norm_gain):
    blocks = TOKENS // SPAN
    x_pad = jnp.pad(x_in, ((CONV - 1, 0), (0, 0)))
    b_pad = jnp.pad(b_in, ((CONV - 1, 0), (0, 0)))
    c_pad = jnp.pad(c_in, ((CONV - 1, 0), (0, 0)))
    decay_rate = jnp.exp(a_log)
    lower = jnp.tril(jnp.ones((SPAN, SPAN), dtype=bool))

    def block_step(state, index):
        start = (index * SPAN).astype(jnp.int32)
        x_act = causal_silu(lax.dynamic_slice_in_dim(x_pad, start, SPAN + CONV - 1, 0), conv_x)
        b_act = causal_silu(lax.dynamic_slice_in_dim(b_pad, start, SPAN + CONV - 1, 0), conv_b)
        c_act = causal_silu(lax.dynamic_slice_in_dim(c_pad, start, SPAN + CONV - 1, 0), conv_c)
        delta = jax.nn.softplus(lax.dynamic_slice_in_dim(dt_raw, start, SPAN, 0) + dt_bias)
        logs = jnp.cumsum(-decay_rate * delta, axis=0)
        heads_x = x_act.reshape(SPAN, HEADS, HEAD_DIM).astype(jnp.float32)
        group_b = b_act.reshape(SPAN, GROUPS, STATE).astype(jnp.float32)
        group_c = c_act.reshape(SPAN, GROUPS, STATE).astype(jnp.float32)
        scores = jnp.einsum('tgn,sgn->gts', group_c, group_b)
        scores = jnp.repeat(scores, HEADS_DEV, axis=0)
        logs_t = logs.T
        gap = jnp.where(lower[None], logs_t[:, :, None] - logs_t[:, None, :], 0.0)
        decay = jnp.where(lower[None], jnp.exp(gap), 0.0)
        weights = rounded(scores * decay * delta.T[:, None, :])
        inner = jnp.einsum('hts,shp->thp', weights, heads_x)
        state_low = rounded(state).reshape(GROUPS, HEADS_DEV, HEAD_DIM, STATE)
        outer = jnp.einsum('tgn,ghpn->tghp', group_c, state_low).reshape(SPAN, HEADS, HEAD_DIM)
        y_val = inner + jnp.exp(logs)[:, :, None] * outer + d_skip[None, :, None] * heads_x
        last = logs[-1]
        scaled = rounded((jnp.exp(last[None, :] - logs) * delta)[:, :, None] * heads_x)
        update = jnp.einsum('sghp,sgn->ghpn', scaled.reshape(SPAN, GROUPS, HEADS_DEV, HEAD_DIM), group_b)
        new_state = jnp.exp(last)[:, None, None] * state + update.reshape(HEADS, HEAD_DIM, STATE)
        z_rows = lax.dynamic_slice_in_dim(z_in, start, SPAN, 0).astype(jnp.float32)
        gated = (y_val.reshape(SPAN, CHANNELS) * jax.nn.silu(z_rows)).reshape(SPAN, GROUPS, HEADS_DEV * HEAD_DIM)
        meansq = lax.optimization_barrier(jnp.mean(gated * gated, axis=-1, keepdims=True))
        normed = (gated * lax.rsqrt(meansq + 1e-05)).reshape(SPAN, CHANNELS) * norm_gain
        return (new_state, normed.astype(jnp.bfloat16))
    start_state = jnp.zeros((HEADS, HEAD_DIM, STATE), jnp.float32)
    _, pieces = lax.scan(block_step, start_state, jnp.arange(blocks, dtype=jnp.int32))
    return pieces.reshape(TOKENS, CHANNELS).T
```

```python
import functools

import jax
import jax.numpy as jnp
from jax import lax
from jax.experimental import pallas as pl
from jax.experimental.pallas import tpu as pltpu
from jax.sharding import PartitionSpec as P

SPAN = 128
LANES = 128
HALO = 16
CHUNKS = 8
EPS = 1e-05
MESH = pl.DeviceIdType.MESH


def conv_silu(pad, taps, count):
    total = taps[0:1] * pad[8 - count + 1 : 8 - count + 1 + SPAN, :]
    for tap in range(1, count):
        start = 8 - count + 1 + tap
        total = total + taps[tap : tap + 1] * pad[start : start + SPAN, :]
    return (total / (1.0 + jnp.exp(-total))).astype(jnp.bfloat16)


def kernel(
    n,
    x_ref,
    z_ref,
    b_ref,
    c_ref,
    dt_ref,
    bias_ref,
    alog_ref,
    skip_ref,
    cx_ref,
    cb_ref,
    cc_ref,
    gain_ref,
    out_ref,
    halo_x,
    halo_b,
    halo_c,
    small,
    pad,
    x_t,
    z_t,
    upd,
    state_in,
    state_out,
    stage,
    recv,
    scale_in,
    scale_out,
    log_rows,
    mix_rows,
    grow_rows,
    last_rows,
    skip_rows,
    cols,
    scores,
    b_act,
    c_act,
    ssq,
    gain_col,
    halo_send,
    halo_recv,
    state_send,
    state_recv,
    out_send,
    out_recv,
    scale_send,
    scale_recv,
):
    width = x_ref.shape[1]
    heads = dt_ref.shape[1]
    head = width // heads
    per_block = LANES // head
    chunk = width // CHUNKS
    blocks = chunk // LANES
    chunk_heads = heads // CHUNKS
    rows = width // n
    parts = chunk // rows
    taps = cx_ref.shape[0]
    me = lax.axis_index("ctx")
    nxt = lax.rem(me + 1, n)

    barrier = pltpu.get_barrier_semaphore()

    def greet(other, carry):
        @pl.when(other != me)
        def _():
            pl.semaphore_signal(barrier, inc=1, device_id={"ctx": other}, device_id_type=MESH)

        return carry

    lax.fori_loop(0, n, greet, 0)

    def halo_copy(index):
        source = (x_ref, b_ref, c_ref)[index]
        target = (halo_x, halo_b, halo_c)[index]
        return pltpu.make_async_remote_copy(
            src_ref=source.at[pl.ds(SPAN - HALO, HALO), :],
            dst_ref=target,
            send_sem=halo_send.at[index],
            recv_sem=halo_recv.at[index],
            device_id={"ctx": nxt},
            device_id_type=MESH,
        )

    def state_copy(k):
        return pltpu.make_async_remote_copy(
            src_ref=state_out.at[k],
            dst_ref=state_in.at[k],
            send_sem=state_send.at[k],
            recv_sem=state_recv.at[k],
            device_id={"ctx": nxt},
            device_id_type=MESH,
        )

    def out_copy(k, part, dest, slot):
        return pltpu.make_async_remote_copy(
            src_ref=stage.at[k, pl.ds(part * rows, rows), :],
            dst_ref=recv.at[slot],
            send_sem=out_send.at[dest],
            recv_sem=out_recv.at[slot],
            device_id={"ctx": dest},
            device_id_type=MESH,
        )

    def scale_copy(dest, slot):
        return pltpu.make_async_remote_copy(
            src_ref=scale_out,
            dst_ref=scale_in.at[slot],
            send_sem=scale_send.at[dest],
            recv_sem=scale_recv.at[slot],
            device_id={"ctx": dest},
            device_id_type=MESH,
        )

    pl.semaphore_wait(barrier, n - 1)

    @pl.when(me < n - 1)
    def _():
        for index in range(3):
            halo_copy(index).start()

    small[...] = jnp.zeros_like(small)
    small[0:SPAN, 0:heads] = dt_ref[...]
    small[SPAN : SPAN + 1, 0:heads] = bias_ref[...]
    small[SPAN + 8 : SPAN + 9, 0:heads] = alog_ref[...]
    small[SPAN + 16 : SPAN + 17, 0:heads] = skip_ref[...]
    raw = small[0:SPAN, :] + small[SPAN : SPAN + 1, :]
    delta = jnp.maximum(raw, 0.0) + jnp.log1p(jnp.exp(-jnp.abs(raw)))
    rate = -jnp.exp(small[SPAN + 8 : SPAN + 9, :]) * delta
    down = lax.broadcasted_iota(jnp.int32, (SPAN, SPAN), 0)
    across = lax.broadcasted_iota(jnp.int32, (SPAN, SPAN), 1)
    lower = jnp.where(across <= down, 1.0, 0.0)
    logs = jnp.dot(
        lower, rate, precision=lax.Precision.HIGHEST, preferred_element_type=jnp.float32
    )
    last = logs[SPAN - 1 : SPAN, :]
    shifted = logs - jnp.log(delta)
    for k in range(CHUNKS):
        cols[k, :, 0:chunk_heads] = shifted[:, k * chunk_heads : (k + 1) * chunk_heads]
    log_rows[...] = logs.T
    grow_rows[...] = jnp.exp(logs).T
    mix_rows[...] = (jnp.exp(last - logs) * delta).T
    last_rows[...] = jnp.broadcast_to(jnp.exp(last), (SPAN, LANES)).T
    skip_rows[...] = jnp.broadcast_to(small[SPAN + 16 : SPAN + 17, :], (SPAN, LANES)).T
    gain_col[...] = jnp.broadcast_to(gain_ref[...], (SPAN, rows)).T
    ssq[...] = jnp.zeros_like(ssq)

    def turn_z(i, carry):
        place = pl.ds(pl.multiple_of(i * LANES, LANES), LANES)
        value = z_ref[:, place].astype(jnp.float32)
        z_t[place, :] = (value / (1.0 + jnp.exp(-value))).T
        return carry

    lax.fori_loop(0, width // LANES, turn_z, 0)

    @pl.when(me > 0)
    def _():
        for index in range(3):
            halo_copy(index).wait_recv()

    @pl.when(me == 0)
    def _():
        halo_x[...] = jnp.zeros_like(halo_x)
        halo_b[...] = jnp.zeros_like(halo_b)
        halo_c[...] = jnp.zeros_like(halo_c)
        state_in[...] = jnp.zeros_like(state_in)

    for source, halo, weights, target in (
        (b_ref, halo_b, cb_ref, b_act),
        (c_ref, halo_c, cc_ref, c_act),
    ):
        pad[0, 0:8, :] = halo[...].astype(jnp.float32)[HALO - 8 :]
        pad[0, 8 : 8 + SPAN, :] = source[...].astype(jnp.float32)
        target[...] = conv_silu(pad.at[0], weights[...], taps)
    overlap = lax.dot_general(
        b_act[...], c_act[...], (((1,), (1,)), ((), ())), preferred_element_type=jnp.float32
    )
    scores[...] = jnp.where(down <= across, overlap, 0.0)

    def head_row(ref, index):
        return jnp.broadcast_to(ref[pl.ds(index, 1), :], (head, LANES))

    def block_rows(ref, k, j):
        first = k * chunk_heads + j * per_block
        return jnp.concatenate([head_row(ref, first + i) for i in range(per_block)], axis=0)

    def updates(k, carry):
        for j in range(blocks):
            place = pl.ds(pl.multiple_of(k * chunk + j * LANES, LANES), LANES)
            pad[j, 0:8, :] = halo_x[:, place].astype(jnp.float32)[HALO - 8 :]
            pad[j, 8 : 8 + SPAN, :] = x_ref[:, place].astype(jnp.float32)
            act = conv_silu(pad.at[j], cx_ref[:, place], taps)
            turned = act.astype(jnp.float32).T
            x_t[place, :] = turned.astype(jnp.bfloat16)
            scaled = (turned * block_rows(mix_rows, k, j)).astype(jnp.bfloat16)
            upd[place, :] = jnp.dot(scaled, b_act[...], preferred_element_type=jnp.float32)

        @pl.when(me == 0)
        def _():
            place = pl.ds(pl.multiple_of(k * chunk, chunk), chunk)
            state_out[k] = upd[place, :].astype(jnp.bfloat16)
            state_copy(k).start()

        return carry

    lax.fori_loop(0, CHUNKS, updates, 0)

    def outputs(k, carry):
        @pl.when(me > 0)
        def _():
            state_copy(k).wait_recv()

        @pl.when((me > 0) & (me < n - 1))
        def _():
            for j in range(blocks):
                place = pl.ds(pl.multiple_of(k * chunk + j * LANES, LANES), LANES)
                entering = state_in[k, j * LANES : (j + 1) * LANES, :].astype(jnp.float32)
                leaving = block_rows(last_rows, k, j) * entering + upd[place, :]
                state_out[k, j * LANES : (j + 1) * LANES, :] = leaving.astype(jnp.bfloat16)
            state_copy(k).start()

        shifts = cols[k]
        squares = ssq[0:1, :]
        for j in range(blocks):
            place = pl.ds(pl.multiple_of(k * chunk + j * LANES, LANES), LANES)
            x_block = x_t[place, :]
            inner = []
            for i in range(per_block):
                which = j * per_block + i
                gap = (
                    log_rows[pl.ds(k * chunk_heads + which, 1), :] - shifts[:, which : which + 1]
                )
                weights = (scores[...] * jnp.exp(gap)).astype(jnp.bfloat16)
                inner.append(
                    jnp.dot(
                        x_block[i * head : (i + 1) * head],
                        weights,
                        preferred_element_type=jnp.float32,
                    )
                )
            outer = lax.dot_general(
                state_in[k, j * LANES : (j + 1) * LANES, :],
                c_act[...],
                (((1,), (1,)), ((), ())),
                preferred_element_type=jnp.float32,
            )
            y_val = (
                jnp.concatenate(inner, axis=0)
                + block_rows(grow_rows, k, j) * outer
                + block_rows(skip_rows, k, j) * x_block.astype(jnp.float32)
            )
            gated = y_val * z_t[place, :]
            squares = squares + jnp.sum(gated * gated, axis=0, keepdims=True)
            stage[k, j * LANES : (j + 1) * LANES, :] = gated.astype(jnp.bfloat16)
        ssq[0:1, :] = squares

        for part in range(parts):
            dest = k * parts + part

            @pl.when(dest != me)
            def _():
                out_copy(k, part, dest, me).start()

            @pl.when(dest == me)
            def _():
                recv[me] = stage[k, part * rows : (part + 1) * rows, :]

        return carry

    lax.fori_loop(0, CHUNKS, outputs, 0)

    scale = jnp.broadcast_to(lax.rsqrt(ssq[0:1, :] / width + EPS), (8, LANES))
    scale_out[...] = scale
    scale_in[me] = scale

    def tell(other, carry):
        @pl.when(other != me)
        def _():
            scale_copy(other, me).start()

        return carry

    lax.fori_loop(0, n, tell, 0)

    def finish(source, carry):
        @pl.when(source != me)
        def _():
            out_copy(0, 0, source, source).wait_recv()
            scale_copy(source, source).wait_recv()

        place = pl.ds(pl.multiple_of(source * SPAN, SPAN), SPAN)
        value = recv[source].astype(jnp.float32) * scale_in[source][0:1, :] * gain_col[...]
        out_ref[:, place] = value.astype(jnp.bfloat16)
        return carry

    lax.fori_loop(0, n, finish, 0)

    @pl.when(me < n - 1)
    def _():
        for index in range(3):
            halo_copy(index).wait_send()

        def drain_state(k, carry):
            state_copy(k).wait_send()
            return carry

        lax.fori_loop(0, CHUNKS, drain_state, 0)

    def drain(other, carry):
        @pl.when(other != me)
        def _():
            out_copy(0, 0, other, me).wait_send()
            scale_copy(other, me).wait_send()

        return carry

    lax.fori_loop(0, n, drain, 0)


def shards(
    x_in, z_in, b_in, c_in, dt_raw, dt_bias, a_log, d_skip, conv_x, conv_b, conv_c, norm_gain
):
    n = lax.axis_size("ctx")
    width = x_in.shape[1]
    state = b_in.shape[1]
    rows = width // n
    chunk = width // CHUNKS
    own_gain = lax.dynamic_slice_in_dim(norm_gain, lax.axis_index("ctx") * rows, rows)
    vmem = pl.BlockSpec(memory_space=pltpu.VMEM)
    f32, bf16 = jnp.float32, jnp.bfloat16
    dma = pltpu.SemaphoreType.DMA
    square = pltpu.VMEM((LANES, LANES), f32)
    return pl.pallas_call(
        functools.partial(kernel, n),
        out_shape=jax.ShapeDtypeStruct((rows, n * SPAN), bf16),
        in_specs=[vmem] * 12,
        out_specs=vmem,
        scratch_shapes=[
            pltpu.VMEM((HALO, width), bf16),
            pltpu.VMEM((HALO, state), bf16),
            pltpu.VMEM((HALO, state), bf16),
            pltpu.VMEM((SPAN + 24, LANES), f32),
            pltpu.VMEM((max(1, chunk // LANES), SPAN + 8, LANES), f32),
            pltpu.VMEM((width, SPAN), bf16),
            pltpu.VMEM((width, SPAN), f32),
            pltpu.VMEM((width, state), f32),
            pltpu.VMEM((CHUNKS, chunk, state), bf16),
            pltpu.VMEM((CHUNKS, chunk, state), bf16),
            pltpu.VMEM((CHUNKS, chunk, SPAN), bf16),
            pltpu.VMEM((n, rows, SPAN), bf16),
            pltpu.VMEM((n, 8, LANES), f32),
            pltpu.VMEM((8, LANES), f32),
            square,
            square,
            square,
            square,
            square,
            pltpu.VMEM((CHUNKS, SPAN, LANES), f32),
            square,
            pltpu.VMEM((SPAN, state), bf16),
            pltpu.VMEM((SPAN, state), bf16),
            pltpu.VMEM((8, LANES), f32),
            pltpu.VMEM((rows, LANES), f32),
            dma((3,)),
            dma((3,)),
            dma((CHUNKS,)),
            dma((CHUNKS,)),
            dma((n,)),
            dma((n,)),
            dma((n,)),
            dma((n,)),
        ],
        compiler_params=pltpu.CompilerParams(
            collective_id=0, has_side_effects=True, vmem_limit_bytes=40 * 1024 * 1024
        ),
        cost_estimate=pl.CostEstimate(
            flops=8 * SPAN * SPAN * width, bytes_accessed=6 * SPAN * width, transcendentals=0
        ),
    )(
        x_in,
        z_in,
        b_in,
        c_in,
        dt_raw,
        dt_bias[None, :],
        a_log[None, :],
        d_skip[None, :],
        conv_x,
        conv_b,
        conv_c,
        own_gain[None, :],
    )


def solution(mesh):
    return jax.shard_map(
        shards,
        mesh=mesh,
        in_specs=(
            P("ctx", "tp"),
            P("ctx", "tp"),
            P("ctx", "tp"),
            P("ctx", "tp"),
            P("ctx", "tp"),
            P("tp"),
            P("tp"),
            P("tp"),
            P(None, "tp"),
            P(None, "tp"),
            P(None, "tp"),
            P("tp"),
        ),
        out_specs=P(("tp", "ctx"), None),
        check_vma=False,
    )
```

```python
import functools

import jax
import jax.numpy as jnp
from jax import lax
from jax.experimental import pallas as pl
from jax.experimental.pallas import tpu as pltpu
from jax.sharding import PartitionSpec as P

SPAN = 128
LANES = 128
HALO = 16
CHUNKS = 8
EPS = 1e-05
MESH = pl.DeviceIdType.MESH


def conv_silu(pad, taps, count):
    total = taps[0:1] * pad[8 - count + 1 : 8 - count + 1 + SPAN, :]
    for tap in range(1, count):
        start = 8 - count + 1 + tap
        total = total + taps[tap : tap + 1] * pad[start : start + SPAN, :]
    return (total / (1.0 + jnp.exp(-total))).astype(jnp.bfloat16)


def kernel(
    n,
    x_ref,
    z_ref,
    b_ref,
    c_ref,
    dt_ref,
    bias_ref,
    alog_ref,
    skip_ref,
    cx_ref,
    cb_ref,
    cc_ref,
    gain_ref,
    out_ref,
    x_buf,
    z_buf,
    b_buf,
    c_buf,
    cx_buf,
    cb_buf,
    cc_buf,
    halo_x,
    halo_b,
    halo_c,
    small,
    pad,
    x_t,
    z_t,
    pre,
    upd,
    state_in,
    state_out,
    stage,
    recv,
    scale_in,
    scale_out,
    log_rows,
    mix_rows,
    grow_rows,
    last_rows,
    skip_rows,
    cols,
    scores,
    b_act,
    c_act,
    ssq,
    gain_col,
    load,
    halo_send,
    halo_recv,
    state_send,
    state_recv,
    out_send,
    out_recv,
    scale_send,
    scale_recv,
):
    width = x_ref.shape[1]
    heads = dt_ref.shape[0]
    head = width // heads
    per_block = LANES // head
    chunk = width // CHUNKS
    blocks = chunk // LANES
    chunk_heads = heads // CHUNKS
    rows = width // n
    parts = chunk // rows
    taps = cx_ref.shape[0]
    me = lax.axis_index("ctx")
    nxt = lax.rem(me + 1, n)

    barrier = pltpu.get_barrier_semaphore()

    def greet(other, carry):
        @pl.when(other != me)
        def _():
            pl.semaphore_signal(barrier, inc=1, device_id={"ctx": other}, device_id_type=MESH)

        return carry

    lax.fori_loop(0, n, greet, 0)

    def halo_copy(index):
        source = (x_ref, b_ref, c_ref)[index]
        target = (halo_x, halo_b, halo_c)[index]
        return pltpu.make_async_remote_copy(
            src_ref=source.at[pl.ds(SPAN - HALO, HALO), :],
            dst_ref=target,
            send_sem=halo_send.at[index],
            recv_sem=halo_recv.at[index],
            device_id={"ctx": nxt},
            device_id_type=MESH,
        )

    def state_copy(k):
        return pltpu.make_async_remote_copy(
            src_ref=state_out.at[k],
            dst_ref=state_in.at[k],
            send_sem=state_send.at[k],
            recv_sem=state_recv.at[k],
            device_id={"ctx": nxt},
            device_id_type=MESH,
        )

    def out_copy(k, part, dest, slot):
        return pltpu.make_async_remote_copy(
            src_ref=stage.at[k, pl.ds(part * rows, rows), :],
            dst_ref=recv.at[slot],
            send_sem=out_send.at[dest],
            recv_sem=out_recv.at[slot],
            device_id={"ctx": dest},
            device_id_type=MESH,
        )

    def scale_copy(dest, slot):
        return pltpu.make_async_remote_copy(
            src_ref=scale_out,
            dst_ref=scale_in.at[slot],
            send_sem=scale_send.at[dest],
            recv_sem=scale_recv.at[slot],
            device_id={"ctx": dest},
            device_id_type=MESH,
        )

    def loading(index):
        source = (x_ref, b_ref, c_ref, cx_ref, cb_ref, cc_ref, z_ref)[index]
        target = (x_buf, b_buf, c_buf, cx_buf, cb_buf, cc_buf, z_buf)[index]
        return pltpu.make_async_copy(source, target, load.at[index])

    for index in range(7):
        loading(index).start()

    def down_columns(row, count):
        return jnp.broadcast_to(row, (SPAN, count)).T

    small[...] = jnp.zeros_like(small)
    small[SPAN : SPAN + 1, 0:heads] = bias_ref[...]
    small[SPAN + 8 : SPAN + 9, 0:heads] = alog_ref[...]
    small[SPAN + 16 : SPAN + 17, 0:heads] = skip_ref[...]
    small[0:heads, :] = dt_ref[...]
    raw = small[0:SPAN, :] + down_columns(small[SPAN : SPAN + 1, :], LANES)
    delta = jnp.maximum(raw, 0.0) + jnp.log1p(jnp.exp(-jnp.abs(raw)))
    rate = -down_columns(jnp.exp(small[SPAN + 8 : SPAN + 9, :]), LANES) * delta
    down = lax.broadcasted_iota(jnp.int32, (SPAN, SPAN), 0)
    across = lax.broadcasted_iota(jnp.int32, (SPAN, SPAN), 1)
    upper = jnp.where(down <= across, 1.0, 0.0)
    logs = jnp.dot(
        rate, upper, precision=lax.Precision.HIGHEST, preferred_element_type=jnp.float32
    )
    last = jnp.broadcast_to(logs[:, SPAN - 1 : SPAN], (SPAN, LANES))
    log_rows[...] = logs
    grow_rows[...] = jnp.exp(logs)
    mix_rows[...] = jnp.exp(last - logs) * delta
    last_rows[...] = jnp.exp(last)
    skip_rows[...] = down_columns(small[SPAN + 16 : SPAN + 17, :], LANES)
    shifted = (logs - jnp.log(delta)).T
    for k in range(CHUNKS):
        cols[k, :, 0:chunk_heads] = shifted[:, k * chunk_heads : (k + 1) * chunk_heads]
    ssq[...] = jnp.zeros_like(ssq)

    pl.semaphore_wait(barrier, n - 1)

    @pl.when(me < n - 1)
    def _():
        for index in range(3):
            halo_copy(index).start()

    if rows % LANES == 0:
        own_gain = gain_ref[:, pl.ds(pl.multiple_of(me * rows, LANES), rows)]
    else:
        own_gain = gain_ref[pl.ds(me, 1), :]
    gain_col[...] = down_columns(own_gain, rows)
    for index in range(6):
        loading(index).wait()

    @pl.when(me > 0)
    def _():
        for index in range(3):
            halo_copy(index).wait_recv()

    @pl.when(me == 0)
    def _():
        halo_x[...] = jnp.zeros_like(halo_x)
        halo_b[...] = jnp.zeros_like(halo_b)
        halo_c[...] = jnp.zeros_like(halo_c)
        state_in[...] = jnp.zeros_like(state_in)

    for index, (source, halo, weights, target) in enumerate(
        ((b_buf, halo_b, cb_buf, b_act), (c_buf, halo_c, cc_buf, c_act))
    ):
        pad[index, 0:8, :] = halo[...].astype(jnp.float32)[HALO - 8 :]
        pad[index, 8 : 8 + SPAN, :] = source[...].astype(jnp.float32)
        target[...] = conv_silu(pad.at[index], weights[...], taps)
    overlap = lax.dot_general(
        b_act[...], c_act[...], (((1,), (1,)), ((), ())), preferred_element_type=jnp.float32
    )
    scores[...] = jnp.where(down <= across, overlap, 0.0)

    def head_row(ref, index):
        return jnp.broadcast_to(ref[pl.ds(index, 1), :], (head, LANES))

    def block_rows(ref, k, j):
        first = k * chunk_heads + j * per_block
        return jnp.concatenate([head_row(ref, first + i) for i in range(per_block)], axis=0)

    def block_place(k, j):
        return pl.ds(pl.multiple_of(k * chunk + j * LANES, LANES), LANES)

    early = me < n // 2

    def forward(k):
        for j in range(blocks):
            entering = state_in[k, j * LANES : (j + 1) * LANES, :].astype(jnp.float32)
            leaving = block_rows(last_rows, k, j) * entering + upd[block_place(k, j), :]
            state_out[k, j * LANES : (j + 1) * LANES, :] = leaving.astype(jnp.bfloat16)
        state_copy(k).start()

    def updates(k, carry):
        for j in range(blocks):
            place = block_place(k, j)
            pad[j, 0:8, :] = halo_x[:, place].astype(jnp.float32)[HALO - 8 :]
            pad[j, 8 : 8 + SPAN, :] = x_buf[:, place].astype(jnp.float32)
            act = conv_silu(pad.at[j], cx_buf[:, place], taps)
            turned = act.astype(jnp.float32).T
            x_t[place, :] = turned.astype(jnp.bfloat16)
            scaled = (turned * block_rows(mix_rows, k, j)).astype(jnp.bfloat16)
            upd[place, :] = jnp.dot(scaled, b_act[...], preferred_element_type=jnp.float32)

        @pl.when(early)
        def _():
            @pl.when(me > 0)
            def _():
                state_copy(k).wait_recv()

            forward(k)

        return carry

    lax.fori_loop(0, CHUNKS, updates, 0)
    loading(6).wait()

    def within(k):
        shifts = cols[k]
        for j in range(blocks):
            place = block_place(k, j)
            value = z_buf[:, place].astype(jnp.float32)
            z_t[place, :] = (value / (1.0 + jnp.exp(-value))).T
            x_block = x_t[place, :]
            inner = []
            for i in range(per_block):
                which = j * per_block + i
                gap = (
                    log_rows[pl.ds(k * chunk_heads + which, 1), :] - shifts[:, which : which + 1]
                )
                weights = (scores[...] * jnp.exp(gap)).astype(jnp.bfloat16)
                inner.append(
                    jnp.dot(
                        x_block[i * head : (i + 1) * head],
                        weights,
                        preferred_element_type=jnp.float32,
                    )
                )
            pre[place, :] = jnp.concatenate(inner, axis=0) + block_rows(
                skip_rows, k, j
            ) * x_block.astype(jnp.float32)

    ahead = jnp.where(early, 0, jnp.minimum(me - n // 2 + 1, CHUNKS))

    def within_ahead(k, carry):
        within(k)
        return carry

    lax.fori_loop(0, ahead, within_ahead, 0)

    def outputs(step, carry):
        k = jnp.where(early, lax.rem(step + CHUNKS // 2, CHUNKS), step)

        @pl.when(step >= ahead)
        def _():
            within(k)

        @pl.when(jnp.logical_not(early))
        def _():
            state_copy(k).wait_recv()

            @pl.when(me < n - 1)
            def _():
                forward(k)

        squares = ssq[0:1, :]
        for j in range(blocks):
            place = block_place(k, j)
            outer = lax.dot_general(
                state_in[k, j * LANES : (j + 1) * LANES, :],
                c_act[...],
                (((1,), (1,)), ((), ())),
                preferred_element_type=jnp.float32,
            )
            gated = (pre[place, :] + block_rows(grow_rows, k, j) * outer) * z_t[place, :]
            squares = squares + jnp.sum(gated * gated, axis=0, keepdims=True)
            stage[k, j * LANES : (j + 1) * LANES, :] = gated.astype(jnp.bfloat16)
        ssq[0:1, :] = squares

        for part in range(parts):
            dest = k * parts + part

            @pl.when(dest != me)
            def _():
                out_copy(k, part, dest, me).start()

            @pl.when(dest == me)
            def _():
                recv[me] = stage[k, part * rows : (part + 1) * rows, :]

        return carry

    lax.fori_loop(0, CHUNKS, outputs, 0)

    scale = jnp.broadcast_to(lax.rsqrt(ssq[0:1, :] / width + EPS), (8, LANES))
    scale_out[...] = scale
    scale_in[me] = scale

    def tell(other, carry):
        @pl.when(other != me)
        def _():
            scale_copy(other, me).start()

        return carry

    lax.fori_loop(0, n, tell, 0)

    def finish(source, carry):
        @pl.when(source != me)
        def _():
            out_copy(0, 0, source, source).wait_recv()
            scale_copy(source, source).wait_recv()

        place = pl.ds(pl.multiple_of(source * SPAN, SPAN), SPAN)
        value = recv[source].astype(jnp.float32) * scale_in[source][0:1, :] * gain_col[...]
        out_ref[:, place] = value.astype(jnp.bfloat16)
        return carry

    lax.fori_loop(0, n, finish, 0)

    @pl.when(me < n - 1)
    def _():
        for index in range(3):
            halo_copy(index).wait_send()

        def drain_state(k, carry):
            state_copy(k).wait_send()
            return carry

        lax.fori_loop(0, CHUNKS, drain_state, 0)

    def drain(other, carry):
        @pl.when(other != me)
        def _():
            out_copy(0, 0, other, me).wait_send()
            scale_copy(other, me).wait_send()

        return carry

    lax.fori_loop(0, n, drain, 0)


def shards(
    x_in, z_in, b_in, c_in, dt_raw, dt_bias, a_log, d_skip, conv_x, conv_b, conv_c, norm_gain
):
    n = lax.axis_size("ctx")
    width = x_in.shape[1]
    state = b_in.shape[1]
    rows = width // n
    chunk = width // CHUNKS
    gain = norm_gain.reshape((1, width) if rows % LANES == 0 else (n, rows))
    taps = conv_x.shape[0]
    hbm = pl.BlockSpec(memory_space=pl.ANY)
    vmem = pl.BlockSpec(memory_space=pltpu.VMEM)
    f32, bf16 = jnp.float32, jnp.bfloat16
    dma = pltpu.SemaphoreType.DMA
    square = pltpu.VMEM((LANES, LANES), f32)
    return pl.pallas_call(
        functools.partial(kernel, n),
        out_shape=jax.ShapeDtypeStruct((rows, n * SPAN), bf16),
        in_specs=[hbm] * 4 + [vmem] * 4 + [hbm] * 3 + [vmem],
        out_specs=vmem,
        scratch_shapes=[
            pltpu.VMEM((SPAN, width), bf16),
            pltpu.VMEM((SPAN, width), bf16),
            pltpu.VMEM((SPAN, state), bf16),
            pltpu.VMEM((SPAN, state), bf16),
            pltpu.VMEM((taps, width), f32),
            pltpu.VMEM((taps, state), f32),
            pltpu.VMEM((taps, state), f32),
            pltpu.VMEM((HALO, width), bf16),
            pltpu.VMEM((HALO, state), bf16),
            pltpu.VMEM((HALO, state), bf16),
            pltpu.VMEM((SPAN + 24, LANES), f32),
            pltpu.VMEM((max(2, chunk // LANES), SPAN + 8, LANES), f32),
            pltpu.VMEM((width, SPAN), bf16),
            pltpu.VMEM((width, SPAN), f32),
            pltpu.VMEM((width, SPAN), f32),
            pltpu.VMEM((width, state), f32),
            pltpu.VMEM((CHUNKS, chunk, state), bf16),
            pltpu.VMEM((CHUNKS, chunk, state), bf16),
            pltpu.VMEM((CHUNKS, chunk, SPAN), bf16),
            pltpu.VMEM((n, rows, SPAN), bf16),
            pltpu.VMEM((n, 8, LANES), f32),
            pltpu.VMEM((8, LANES), f32),
            square,
            square,
            square,
            square,
            square,
            pltpu.VMEM((CHUNKS, SPAN, LANES), f32),
            square,
            pltpu.VMEM((SPAN, state), bf16),
            pltpu.VMEM((SPAN, state), bf16),
            pltpu.VMEM((8, LANES), f32),
            pltpu.VMEM((rows, LANES), f32),
            dma((7,)),
            dma((3,)),
            dma((3,)),
            dma((CHUNKS,)),
            dma((CHUNKS,)),
            dma((n,)),
            dma((n,)),
            dma((n,)),
            dma((n,)),
        ],
        compiler_params=pltpu.CompilerParams(
            collective_id=0, has_side_effects=True, vmem_limit_bytes=56 * 1024 * 1024
        ),
        cost_estimate=pl.CostEstimate(
            flops=8 * SPAN * SPAN * width, bytes_accessed=6 * SPAN * width, transcendentals=0
        ),
    )(
        x_in,
        z_in,
        b_in,
        c_in,
        dt_raw.T,
        dt_bias[None, :],
        a_log[None, :],
        d_skip[None, :],
        conv_x,
        conv_b,
        conv_c,
        gain,
    )


def solution(mesh):
    return jax.shard_map(
        shards,
        mesh=mesh,
        in_specs=(
            P("ctx", "tp"),
            P("ctx", "tp"),
            P("ctx", "tp"),
            P("ctx", "tp"),
            P("ctx", "tp"),
            P("tp"),
            P("tp"),
            P("tp"),
            P(None, "tp"),
            P(None, "tp"),
            P(None, "tp"),
            P("tp"),
        ),
        out_specs=P(("tp", "ctx"), None),
        check_vma=False,
    )
```

```python
import functools

import jax
import jax.numpy as jnp
from jax import lax
from jax.experimental import pallas as pl
from jax.experimental.pallas import tpu as pltpu
from jax.sharding import PartitionSpec as P

SPAN = 128
LANES = 128
HALO = 16
CHUNKS = 8
EPS = 1e-05
LOG2E = 1.4426950408889634
MESH = pl.DeviceIdType.MESH


def silu(value):
    half = 0.5 * value
    return half + half * jnp.tanh(half)


def conv_silu(pad, taps, count):
    total = taps[0:1] * pad[8 - count + 1 : 8 - count + 1 + SPAN, :]
    for tap in range(1, count):
        start = 8 - count + 1 + tap
        total = total + taps[tap : tap + 1] * pad[start : start + SPAN, :]
    return silu(total).astype(jnp.bfloat16)


def kernel(
    n,
    x_ref,
    z_ref,
    b_ref,
    c_ref,
    dt_ref,
    bias_ref,
    alog_ref,
    skip_ref,
    cx_ref,
    cb_ref,
    cc_ref,
    recv,
    scale_in,
    x_buf,
    z_buf,
    b_buf,
    c_buf,
    cx_buf,
    cb_buf,
    cc_buf,
    halo_x,
    halo_b,
    halo_c,
    small,
    pad,
    x_t,
    z_t,
    pre,
    upd,
    state_in,
    state_out,
    stage,
    scale_out,
    log_rows,
    mix_rows,
    grow_rows,
    last_rows,
    skip_rows,
    cols,
    scores,
    b_act,
    c_act,
    ssq,
    load,
    halo_send,
    halo_recv,
    state_send,
    state_recv,
    out_send,
    out_recv,
    scale_send,
    scale_recv,
):
    width = x_ref.shape[1]
    heads = dt_ref.shape[0]
    head = width // heads
    per_block = LANES // head
    chunk = width // CHUNKS
    blocks = chunk // LANES
    chunk_heads = heads // CHUNKS
    rows = width // n
    parts = chunk // rows
    taps = cx_ref.shape[0]
    me = lax.axis_index("ctx")
    nxt = lax.rem(me + 1, n)

    barrier = pltpu.get_barrier_semaphore()

    def greet(other, carry):
        @pl.when(other != me)
        def _():
            pl.semaphore_signal(barrier, inc=1, device_id={"ctx": other}, device_id_type=MESH)

        return carry

    lax.fori_loop(0, n, greet, 0)

    def halo_copy(index):
        source = (x_ref, b_ref, c_ref)[index]
        target = (halo_x, halo_b, halo_c)[index]
        return pltpu.make_async_remote_copy(
            src_ref=source.at[pl.ds(SPAN - HALO, HALO), :],
            dst_ref=target,
            send_sem=halo_send.at[index],
            recv_sem=halo_recv.at[index],
            device_id={"ctx": nxt},
            device_id_type=MESH,
        )

    def state_copy(k):
        return pltpu.make_async_remote_copy(
            src_ref=state_out.at[k],
            dst_ref=state_in.at[k],
            send_sem=state_send.at[k],
            recv_sem=state_recv.at[k],
            device_id={"ctx": nxt},
            device_id_type=MESH,
        )

    def out_copy(k, part, dest, slot):
        return pltpu.make_async_remote_copy(
            src_ref=stage.at[k, pl.ds(part * rows, rows), :],
            dst_ref=recv.at[slot],
            send_sem=out_send.at[dest],
            recv_sem=out_recv.at[slot],
            device_id={"ctx": dest},
            device_id_type=MESH,
        )

    def own_out(k, part):
        return pltpu.make_async_copy(
            stage.at[k, pl.ds(part * rows, rows), :], recv.at[me], out_recv.at[me]
        )

    def own_scale():
        return pltpu.make_async_copy(scale_out, scale_in.at[me], scale_recv.at[me])

    def scale_copy(dest, slot):
        return pltpu.make_async_remote_copy(
            src_ref=scale_out,
            dst_ref=scale_in.at[slot],
            send_sem=scale_send.at[dest],
            recv_sem=scale_recv.at[slot],
            device_id={"ctx": dest},
            device_id_type=MESH,
        )

    def loading(index):
        source = (x_ref, b_ref, c_ref, cx_ref, cb_ref, cc_ref, z_ref)[index]
        target = (x_buf, b_buf, c_buf, cx_buf, cb_buf, cc_buf, z_buf)[index]
        return pltpu.make_async_copy(source, target, load.at[index])

    for index in range(7):
        loading(index).start()

    def down_columns(row, count):
        return jnp.broadcast_to(row, (SPAN, count)).T

    small[...] = jnp.zeros_like(small)
    small[SPAN : SPAN + 1, 0:heads] = bias_ref[...]
    small[SPAN + 8 : SPAN + 9, 0:heads] = alog_ref[...]
    small[SPAN + 16 : SPAN + 17, 0:heads] = skip_ref[...]
    small[0:heads, :] = dt_ref[...]
    raw = small[0:SPAN, :] + down_columns(small[SPAN : SPAN + 1, :], LANES)
    delta = jnp.maximum(raw, 0.0) + jnp.log1p(jnp.exp(-jnp.abs(raw)))
    rate = -down_columns(jnp.exp(small[SPAN + 8 : SPAN + 9, :]), LANES) * delta
    down = lax.broadcasted_iota(jnp.int32, (SPAN, SPAN), 0)
    across = lax.broadcasted_iota(jnp.int32, (SPAN, SPAN), 1)
    upper = jnp.where(down <= across, 1.0, 0.0)
    logs = jnp.dot(
        rate, upper, precision=lax.Precision.HIGHEST, preferred_element_type=jnp.float32
    )
    last = jnp.broadcast_to(logs[:, SPAN - 1 : SPAN], (SPAN, LANES))
    log_rows[...] = logs * LOG2E
    grow_rows[...] = jnp.exp(logs)
    mix_rows[...] = jnp.exp(last - logs) * delta
    last_rows[...] = jnp.exp(last)
    skip_rows[...] = down_columns(small[SPAN + 16 : SPAN + 17, :], LANES)
    shifted = ((logs - jnp.log(delta)) * LOG2E).T
    for k in range(CHUNKS):
        cols[k, :, 0:chunk_heads] = shifted[:, k * chunk_heads : (k + 1) * chunk_heads]
    ssq[...] = jnp.zeros_like(ssq)

    pl.semaphore_wait(barrier, n - 1)

    @pl.when(me < n - 1)
    def _():
        for index in range(3):
            halo_copy(index).start()

    for index in range(6):
        loading(index).wait()

    @pl.when(me > 0)
    def _():
        for index in range(3):
            halo_copy(index).wait_recv()

    @pl.when(me == 0)
    def _():
        halo_x[...] = jnp.zeros_like(halo_x)
        halo_b[...] = jnp.zeros_like(halo_b)
        halo_c[...] = jnp.zeros_like(halo_c)
        state_in[...] = jnp.zeros_like(state_in)

    for index, (source, halo, weights, target) in enumerate(
        ((b_buf, halo_b, cb_buf, b_act), (c_buf, halo_c, cc_buf, c_act))
    ):
        pad[index, 0:8, :] = halo[...].astype(jnp.float32)[HALO - 8 :]
        pad[index, 8 : 8 + SPAN, :] = source[...].astype(jnp.float32)
        target[...] = conv_silu(pad.at[index], weights[...], taps)
    overlap = lax.dot_general(
        b_act[...], c_act[...], (((1,), (1,)), ((), ())), preferred_element_type=jnp.float32
    )
    scores[...] = jnp.where(down <= across, overlap, 0.0)

    def head_row(ref, index):
        return jnp.broadcast_to(ref[pl.ds(index, 1), :], (head, LANES))

    def block_rows(ref, k, j):
        first = k * chunk_heads + j * per_block
        return jnp.concatenate([head_row(ref, first + i) for i in range(per_block)], axis=0)

    def block_place(k, j):
        return pl.ds(pl.multiple_of(k * chunk + j * LANES, LANES), LANES)

    early = me < n // 2

    def forward(k):
        for j in range(blocks):
            entering = state_in[k, j * LANES : (j + 1) * LANES, :].astype(jnp.float32)
            leaving = block_rows(last_rows, k, j) * entering + upd[block_place(k, j), :]
            state_out[k, j * LANES : (j + 1) * LANES, :] = leaving.astype(jnp.bfloat16)
        state_copy(k).start()

    def updates(k, carry):
        for j in range(blocks):
            place = block_place(k, j)
            pad[j, 0:8, :] = halo_x[:, place].astype(jnp.float32)[HALO - 8 :]
            pad[j, 8 : 8 + SPAN, :] = x_buf[:, place].astype(jnp.float32)
            act = conv_silu(pad.at[j], cx_buf[:, place], taps)
            turned = act.T
            x_t[place, :] = turned
            scaled = (turned.astype(jnp.float32) * block_rows(mix_rows, k, j)).astype(jnp.bfloat16)
            upd[place, :] = jnp.dot(scaled, b_act[...], preferred_element_type=jnp.float32)

        @pl.when(early)
        def _():
            @pl.when(me > 0)
            def _():
                state_copy(k).wait_recv()

            forward(k)

        return carry

    lax.fori_loop(0, CHUNKS, updates, 0)
    loading(6).wait()

    def within(k):
        shifts = cols[k]
        for j in range(blocks):
            place = block_place(k, j)
            z_t[place, :] = silu(z_buf[:, place].T.astype(jnp.float32))
            x_block = x_t[place, :]
            inner = []
            for i in range(per_block):
                which = j * per_block + i
                gap = (
                    log_rows[pl.ds(k * chunk_heads + which, 1), :] - shifts[:, which : which + 1]
                )
                weights = (scores[...] * jnp.exp2(gap)).astype(jnp.bfloat16)
                inner.append(
                    jnp.dot(
                        x_block[i * head : (i + 1) * head],
                        weights,
                        preferred_element_type=jnp.float32,
                    )
                )
            pre[place, :] = jnp.concatenate(inner, axis=0) + block_rows(
                skip_rows, k, j
            ) * x_block.astype(jnp.float32)

    ahead = jnp.where(early, 0, jnp.minimum(2 * (me - n // 2) + 2, CHUNKS))

    def within_ahead(k, carry):
        within(k)
        return carry

    lax.fori_loop(0, ahead, within_ahead, 0)

    def outputs(step, carry):
        k = jnp.where(early, lax.rem(step + CHUNKS // 2, CHUNKS), step)

        @pl.when(step >= ahead)
        def _():
            within(k)

        @pl.when(jnp.logical_not(early))
        def _():
            state_copy(k).wait_recv()

            @pl.when(me < n - 1)
            def _():
                forward(k)

        squares = ssq[0:1, :]
        for j in range(blocks):
            place = block_place(k, j)
            outer = lax.dot_general(
                state_in[k, j * LANES : (j + 1) * LANES, :],
                c_act[...],
                (((1,), (1,)), ((), ())),
                preferred_element_type=jnp.float32,
            )
            gated = (pre[place, :] + block_rows(grow_rows, k, j) * outer) * z_t[place, :]
            squares = squares + jnp.sum(gated * gated, axis=0, keepdims=True)
            stage[k, j * LANES : (j + 1) * LANES, :] = gated.astype(jnp.bfloat16)
        ssq[0:1, :] = squares

        for part in range(parts):
            dest = k * parts + part

            @pl.when(dest != me)
            def _():
                out_copy(k, part, dest, me).start()

            @pl.when(dest == me)
            def _():
                own_out(k, part).start()

        return carry

    lax.fori_loop(0, CHUNKS, outputs, 0)

    scale = jnp.broadcast_to(lax.rsqrt(ssq[0:1, :] / width + EPS), (8, LANES))
    scale_out[...] = scale
    own_scale().start()

    def tell(other, carry):
        @pl.when(other != me)
        def _():
            scale_copy(other, me).start()

        return carry

    lax.fori_loop(0, n, tell, 0)

    def finish(source, carry):
        @pl.when(source != me)
        def _():
            out_copy(0, 0, source, source).wait_recv()
            scale_copy(source, source).wait_recv()

        @pl.when(source == me)
        def _():
            own_out(0, 0).wait()
            own_scale().wait()

        return carry

    lax.fori_loop(0, n, finish, 0)

    @pl.when(me < n - 1)
    def _():
        for index in range(3):
            halo_copy(index).wait_send()

        def drain_state(k, carry):
            state_copy(k).wait_send()
            return carry

        lax.fori_loop(0, CHUNKS, drain_state, 0)

    def drain(other, carry):
        @pl.when(other != me)
        def _():
            out_copy(0, 0, other, me).wait_send()
            scale_copy(other, me).wait_send()

        return carry

    lax.fori_loop(0, n, drain, 0)


def normalise(gated_ref, scale_ref, gain_ref, out_ref, gain_col):
    rows = out_ref.shape[0]
    me = lax.axis_index("ctx")

    @pl.when(pl.program_id(0) == 0)
    def _():
        if rows % LANES == 0:
            own = gain_ref[:, pl.ds(pl.multiple_of(me * rows, LANES), rows)]
        else:
            own = gain_ref[pl.ds(me, 1), :]
        gain_col[...] = jnp.broadcast_to(own, (LANES, rows)).T

    value = gated_ref[0].astype(jnp.float32) * scale_ref[0, 0:1, :] * gain_col[...]
    out_ref[...] = value.astype(jnp.bfloat16)


def shards(
    x_in, z_in, b_in, c_in, dt_raw, dt_bias, a_log, d_skip, conv_x, conv_b, conv_c, norm_gain
):
    n = lax.axis_size("ctx")
    width = x_in.shape[1]
    state = b_in.shape[1]
    rows = width // n
    chunk = width // CHUNKS
    gain = norm_gain.reshape((1, width) if rows % LANES == 0 else (n, rows))
    taps = conv_x.shape[0]
    hbm = pl.BlockSpec(memory_space=pl.ANY)
    vmem = pl.BlockSpec(memory_space=pltpu.VMEM)
    f32, bf16 = jnp.float32, jnp.bfloat16
    dma = pltpu.SemaphoreType.DMA
    square = pltpu.VMEM((LANES, LANES), f32)
    gated, scales = pl.pallas_call(
        functools.partial(kernel, n),
        out_shape=(
            jax.ShapeDtypeStruct((n, rows, SPAN), bf16),
            jax.ShapeDtypeStruct((n, 8, LANES), f32),
        ),
        in_specs=[hbm] * 4 + [vmem] * 4 + [hbm] * 3,
        out_specs=(hbm, hbm),
        scratch_shapes=[
            pltpu.VMEM((SPAN, width), bf16),
            pltpu.VMEM((SPAN, width), bf16),
            pltpu.VMEM((SPAN, state), bf16),
            pltpu.VMEM((SPAN, state), bf16),
            pltpu.VMEM((taps, width), f32),
            pltpu.VMEM((taps, state), f32),
            pltpu.VMEM((taps, state), f32),
            pltpu.VMEM((HALO, width), bf16),
            pltpu.VMEM((HALO, state), bf16),
            pltpu.VMEM((HALO, state), bf16),
            pltpu.VMEM((SPAN + 24, LANES), f32),
            pltpu.VMEM((max(2, chunk // LANES), SPAN + 8, LANES), f32),
            pltpu.VMEM((width, SPAN), bf16),
            pltpu.VMEM((width, SPAN), f32),
            pltpu.VMEM((width, SPAN), f32),
            pltpu.VMEM((width, state), f32),
            pltpu.VMEM((CHUNKS, chunk, state), bf16),
            pltpu.VMEM((CHUNKS, chunk, state), bf16),
            pltpu.VMEM((CHUNKS, chunk, SPAN), bf16),
            pltpu.VMEM((8, LANES), f32),
            square,
            square,
            square,
            square,
            square,
            pltpu.VMEM((CHUNKS, SPAN, LANES), f32),
            square,
            pltpu.VMEM((SPAN, state), bf16),
            pltpu.VMEM((SPAN, state), bf16),
            pltpu.VMEM((8, LANES), f32),
            dma((7,)),
            dma((3,)),
            dma((3,)),
            dma((CHUNKS,)),
            dma((CHUNKS,)),
            dma((n,)),
            dma((n,)),
            dma((n,)),
            dma((n,)),
        ],
        compiler_params=pltpu.CompilerParams(
            collective_id=0, has_side_effects=True, vmem_limit_bytes=56 * 1024 * 1024
        ),
        cost_estimate=pl.CostEstimate(
            flops=8 * SPAN * SPAN * width, bytes_accessed=6 * SPAN * width, transcendentals=0
        ),
    )(
        x_in,
        z_in,
        b_in,
        c_in,
        dt_raw.T,
        dt_bias[None, :],
        a_log[None, :],
        d_skip[None, :],
        conv_x,
        conv_b,
        conv_c,
    )
    return pl.pallas_call(
        normalise,
        grid=(n,),
        out_shape=jax.ShapeDtypeStruct((rows, n * SPAN), bf16),
        in_specs=[
            pl.BlockSpec((1, rows, SPAN), lambda i: (i, 0, 0)),
            pl.BlockSpec((1, 8, LANES), lambda i: (i, 0, 0)),
            pl.BlockSpec(gain.shape, lambda i: (0, 0)),
        ],
        out_specs=pl.BlockSpec((rows, SPAN), lambda i: (0, i)),
        scratch_shapes=[pltpu.VMEM((rows, LANES), f32)],
        compiler_params=pltpu.CompilerParams(vmem_limit_bytes=56 * 1024 * 1024),
    )(gated, scales, gain)


def solution(mesh):
    return jax.shard_map(
        shards,
        mesh=mesh,
        in_specs=(
            P("ctx", "tp"),
            P("ctx", "tp"),
            P("ctx", "tp"),
            P("ctx", "tp"),
            P("ctx", "tp"),
            P("tp"),
            P("tp"),
            P("tp"),
            P(None, "tp"),
            P(None, "tp"),
            P(None, "tp"),
            P("tp"),
        ),
        out_specs=P(("tp", "ctx"), None),
        check_vma=False,
    )
```

```python
import functools

import jax
import jax.numpy as jnp
from jax import lax
from jax.experimental import pallas as pl
from jax.experimental.pallas import tpu as pltpu
from jax.sharding import PartitionSpec as P

SPAN = 128
LANES = 128
HALO = 16
CHUNKS = 8
EPS = 1e-05
LOG2E = 1.4426950408889634
MESH = pl.DeviceIdType.MESH


def silu(value):
    half = 0.5 * value
    return half + half * jnp.tanh(half)


def conv_silu(pad, taps, count):
    total = taps[0:1] * pad[8 - count + 1 : 8 - count + 1 + SPAN, :]
    for tap in range(1, count):
        start = 8 - count + 1 + tap
        total = total + taps[tap : tap + 1] * pad[start : start + SPAN, :]
    return silu(total).astype(jnp.bfloat16)


def kernel(
    n,
    x_ref,
    z_ref,
    b_ref,
    c_ref,
    dt_ref,
    bias_ref,
    alog_ref,
    skip_ref,
    cx_ref,
    cb_ref,
    cc_ref,
    gain_ref,
    out_ref,
    x_buf,
    z_buf,
    b_buf,
    c_buf,
    cx_buf,
    cb_buf,
    cc_buf,
    halo_x,
    halo_b,
    halo_c,
    small,
    pad,
    x_t,
    z_t,
    pre,
    upd,
    state_in,
    state_out,
    stage,
    recv,
    scale_in,
    scale_out,
    log_rows,
    mix_rows,
    grow_rows,
    last_rows,
    skip_rows,
    cols,
    scores,
    b_act,
    c_act,
    ssq,
    gain_col,
    load,
    halo_send,
    halo_recv,
    state_send,
    state_recv,
    out_send,
    out_recv,
    scale_send,
    scale_recv,
):
    width = x_ref.shape[1]
    heads = dt_ref.shape[0]
    head = width // heads
    per_block = LANES // head
    chunk = width // CHUNKS
    blocks = chunk // LANES
    chunk_heads = heads // CHUNKS
    rows = width // n
    parts = chunk // rows
    taps = cx_ref.shape[0]
    me = lax.axis_index("ctx")
    nxt = lax.rem(me + 1, n)

    barrier = pltpu.get_barrier_semaphore()

    def greet(other, carry):
        @pl.when(other != me)
        def _():
            pl.semaphore_signal(barrier, inc=1, device_id={"ctx": other}, device_id_type=MESH)

        return carry

    lax.fori_loop(0, n, greet, 0)

    def halo_copy(index):
        source = (x_ref, b_ref, c_ref)[index]
        target = (halo_x, halo_b, halo_c)[index]
        return pltpu.make_async_remote_copy(
            src_ref=source.at[pl.ds(SPAN - HALO, HALO), :],
            dst_ref=target,
            send_sem=halo_send.at[index],
            recv_sem=halo_recv.at[index],
            device_id={"ctx": nxt},
            device_id_type=MESH,
        )

    def state_copy(k):
        return pltpu.make_async_remote_copy(
            src_ref=state_out.at[k],
            dst_ref=state_in.at[k],
            send_sem=state_send.at[k],
            recv_sem=state_recv.at[k],
            device_id={"ctx": nxt},
            device_id_type=MESH,
        )

    def out_copy(k, part, dest, slot):
        return pltpu.make_async_remote_copy(
            src_ref=stage.at[k, pl.ds(part * rows, rows), :],
            dst_ref=recv.at[slot],
            send_sem=out_send.at[dest],
            recv_sem=out_recv.at[slot],
            device_id={"ctx": dest},
            device_id_type=MESH,
        )

    def scale_copy(dest, slot):
        return pltpu.make_async_remote_copy(
            src_ref=scale_out,
            dst_ref=scale_in.at[slot],
            send_sem=scale_send.at[dest],
            recv_sem=scale_recv.at[slot],
            device_id={"ctx": dest},
            device_id_type=MESH,
        )

    def loading(index):
        source = (x_ref, b_ref, c_ref, cx_ref, cb_ref, cc_ref, z_ref)[index]
        target = (x_buf, b_buf, c_buf, cx_buf, cb_buf, cc_buf, z_buf)[index]
        return pltpu.make_async_copy(source, target, load.at[index])

    for index in range(7):
        loading(index).start()

    def down_columns(row, count):
        return jnp.broadcast_to(row, (SPAN, count)).T

    small[...] = jnp.zeros_like(small)
    small[SPAN : SPAN + 1, 0:heads] = bias_ref[...]
    small[SPAN + 8 : SPAN + 9, 0:heads] = alog_ref[...]
    small[SPAN + 16 : SPAN + 17, 0:heads] = skip_ref[...]
    small[0:heads, :] = dt_ref[...]
    raw = small[0:SPAN, :] + down_columns(small[SPAN : SPAN + 1, :], LANES)
    delta = jnp.maximum(raw, 0.0) + jnp.log1p(jnp.exp(-jnp.abs(raw)))
    rate = -down_columns(jnp.exp(small[SPAN + 8 : SPAN + 9, :]), LANES) * delta
    down = lax.broadcasted_iota(jnp.int32, (SPAN, SPAN), 0)
    across = lax.broadcasted_iota(jnp.int32, (SPAN, SPAN), 1)
    upper = jnp.where(down <= across, 1.0, 0.0)
    logs = jnp.dot(
        rate, upper, precision=lax.Precision.HIGHEST, preferred_element_type=jnp.float32
    )
    last = jnp.broadcast_to(logs[:, SPAN - 1 : SPAN], (SPAN, LANES))
    log_rows[...] = logs * LOG2E
    grow_rows[...] = jnp.exp(logs)
    mix_rows[...] = jnp.exp(last - logs) * delta
    last_rows[...] = jnp.exp(last)
    skip_rows[...] = down_columns(small[SPAN + 16 : SPAN + 17, :], LANES)
    shifted = ((logs - jnp.log(delta)) * LOG2E).T
    for k in range(CHUNKS):
        cols[k, :, 0:chunk_heads] = shifted[:, k * chunk_heads : (k + 1) * chunk_heads]
    ssq[...] = jnp.zeros_like(ssq)

    pl.semaphore_wait(barrier, n - 1)

    @pl.when(me < n - 1)
    def _():
        for index in range(3):
            halo_copy(index).start()

    if rows % LANES == 0:
        own_gain = gain_ref[:, pl.ds(pl.multiple_of(me * rows, LANES), rows)]
    else:
        own_gain = gain_ref[pl.ds(me, 1), :]
    gain_col[...] = down_columns(own_gain, rows)
    for index in range(6):
        loading(index).wait()

    @pl.when(me > 0)
    def _():
        for index in range(3):
            halo_copy(index).wait_recv()

    @pl.when(me == 0)
    def _():
        halo_x[...] = jnp.zeros_like(halo_x)
        halo_b[...] = jnp.zeros_like(halo_b)
        halo_c[...] = jnp.zeros_like(halo_c)
        state_in[...] = jnp.zeros_like(state_in)

    for index, (source, halo, weights, target) in enumerate(
        ((b_buf, halo_b, cb_buf, b_act), (c_buf, halo_c, cc_buf, c_act))
    ):
        pad[index, 0:8, :] = halo[...].astype(jnp.float32)[HALO - 8 :]
        pad[index, 8 : 8 + SPAN, :] = source[...].astype(jnp.float32)
        target[...] = conv_silu(pad.at[index], weights[...], taps)
    overlap = lax.dot_general(
        b_act[...], c_act[...], (((1,), (1,)), ((), ())), preferred_element_type=jnp.float32
    )
    scores[...] = jnp.where(down <= across, overlap, 0.0)

    def head_row(ref, index):
        return jnp.broadcast_to(ref[pl.ds(index, 1), :], (head, LANES))

    def block_rows(ref, k, j):
        first = k * chunk_heads + j * per_block
        return jnp.concatenate([head_row(ref, first + i) for i in range(per_block)], axis=0)

    def block_place(k, j):
        return pl.ds(pl.multiple_of(k * chunk + j * LANES, LANES), LANES)

    early = me < n // 2

    def forward(k):
        for j in range(blocks):
            entering = state_in[k, j * LANES : (j + 1) * LANES, :].astype(jnp.float32)
            leaving = block_rows(last_rows, k, j) * entering + upd[block_place(k, j), :]
            state_out[k, j * LANES : (j + 1) * LANES, :] = leaving.astype(jnp.bfloat16)
        state_copy(k).start()

    def updates(k, carry):
        for j in range(blocks):
            place = block_place(k, j)
            pad[j, 0:8, :] = halo_x[:, place].astype(jnp.float32)[HALO - 8 :]
            pad[j, 8 : 8 + SPAN, :] = x_buf[:, place].astype(jnp.float32)
            act = conv_silu(pad.at[j], cx_buf[:, place], taps)
            turned = act.T
            x_t[place, :] = turned
            scaled = (turned.astype(jnp.float32) * block_rows(mix_rows, k, j)).astype(jnp.bfloat16)
            upd[place, :] = jnp.dot(scaled, b_act[...], preferred_element_type=jnp.float32)

        @pl.when(early)
        def _():
            @pl.when(me > 0)
            def _():
                state_copy(k).wait_recv()

            forward(k)

        return carry

    lax.fori_loop(0, CHUNKS, updates, 0)
    loading(6).wait()

    def within(k):
        shifts = cols[k]
        for j in range(blocks):
            place = block_place(k, j)
            z_t[place, :] = silu(z_buf[:, place].T.astype(jnp.float32))
            x_block = x_t[place, :]
            inner = []
            for i in range(per_block):
                which = j * per_block + i
                gap = (
                    log_rows[pl.ds(k * chunk_heads + which, 1), :] - shifts[:, which : which + 1]
                )
                weights = (scores[...] * jnp.exp2(gap)).astype(jnp.bfloat16)
                inner.append(
                    jnp.dot(
                        x_block[i * head : (i + 1) * head],
                        weights,
                        preferred_element_type=jnp.float32,
                    )
                )
            pre[place, :] = jnp.concatenate(inner, axis=0) + block_rows(
                skip_rows, k, j
            ) * x_block.astype(jnp.float32)

    ahead = jnp.where(early, 0, jnp.minimum(2 * (me - n // 2) + 2, CHUNKS))

    def within_ahead(k, carry):
        within(k)
        return carry

    lax.fori_loop(0, ahead, within_ahead, 0)

    def outputs(k, carry):
        @pl.when(k >= ahead)
        def _():
            within(k)

        @pl.when(jnp.logical_not(early))
        def _():
            state_copy(k).wait_recv()

            @pl.when(me < n - 1)
            def _():
                forward(k)

        squares = ssq[0:1, :]
        for j in range(blocks):
            place = block_place(k, j)
            outer = lax.dot_general(
                state_in[k, j * LANES : (j + 1) * LANES, :],
                c_act[...],
                (((1,), (1,)), ((), ())),
                preferred_element_type=jnp.float32,
            )
            gated = (pre[place, :] + block_rows(grow_rows, k, j) * outer) * z_t[place, :]
            squares = squares + jnp.sum(gated * gated, axis=0, keepdims=True)
            stage[k, j * LANES : (j + 1) * LANES, :] = gated.astype(jnp.bfloat16)
        ssq[0:1, :] = squares

        for part in range(parts):
            dest = k * parts + part

            @pl.when(dest != me)
            def _():
                out_copy(k, part, dest, me).start()

            @pl.when(dest == me)
            def _():
                recv[me] = stage[k, part * rows : (part + 1) * rows, :]

        return carry

    lax.fori_loop(0, CHUNKS, outputs, 0)

    scale = jnp.broadcast_to(lax.rsqrt(ssq[0:1, :] / width + EPS), (8, LANES))
    scale_out[...] = scale
    scale_in[me] = scale

    def tell(other, carry):
        @pl.when(other != me)
        def _():
            scale_copy(other, me).start()

        return carry

    lax.fori_loop(0, n, tell, 0)

    def finish(source, carry):
        @pl.when(source != me)
        def _():
            out_copy(0, 0, source, source).wait_recv()
            scale_copy(source, source).wait_recv()

        place = pl.ds(pl.multiple_of(source * SPAN, SPAN), SPAN)
        value = recv[source].astype(jnp.float32) * scale_in[source][0:1, :] * gain_col[...]
        out_ref[:, place] = value.astype(jnp.bfloat16)
        return carry

    lax.fori_loop(0, n, finish, 0)

    @pl.when(me < n - 1)
    def _():
        for index in range(3):
            halo_copy(index).wait_send()

        def drain_state(k, carry):
            state_copy(k).wait_send()
            return carry

        lax.fori_loop(0, CHUNKS, drain_state, 0)

    def drain(other, carry):
        @pl.when(other != me)
        def _():
            out_copy(0, 0, other, me).wait_send()
            scale_copy(other, me).wait_send()

        return carry

    lax.fori_loop(0, n, drain, 0)


def shards(
    x_in, z_in, b_in, c_in, dt_raw, dt_bias, a_log, d_skip, conv_x, conv_b, conv_c, norm_gain
):
    n = lax.axis_size("ctx")
    width = x_in.shape[1]
    state = b_in.shape[1]
    rows = width // n
    chunk = width // CHUNKS
    gain = norm_gain.reshape((1, width) if rows % LANES == 0 else (n, rows))
    taps = conv_x.shape[0]
    hbm = pl.BlockSpec(memory_space=pl.ANY)
    vmem = pl.BlockSpec(memory_space=pltpu.VMEM)
    f32, bf16 = jnp.float32, jnp.bfloat16
    dma = pltpu.SemaphoreType.DMA
    square = pltpu.VMEM((LANES, LANES), f32)
    return pl.pallas_call(
        functools.partial(kernel, n),
        out_shape=jax.ShapeDtypeStruct((rows, n * SPAN), bf16),
        in_specs=[hbm] * 4 + [vmem] * 4 + [hbm] * 3 + [vmem],
        out_specs=vmem,
        scratch_shapes=[
            pltpu.VMEM((SPAN, width), bf16),
            pltpu.VMEM((SPAN, width), bf16),
            pltpu.VMEM((SPAN, state), bf16),
            pltpu.VMEM((SPAN, state), bf16),
            pltpu.VMEM((taps, width), f32),
            pltpu.VMEM((taps, state), f32),
            pltpu.VMEM((taps, state), f32),
            pltpu.VMEM((HALO, width), bf16),
            pltpu.VMEM((HALO, state), bf16),
            pltpu.VMEM((HALO, state), bf16),
            pltpu.VMEM((SPAN + 24, LANES), f32),
            pltpu.VMEM((max(2, chunk // LANES), SPAN + 8, LANES), f32),
            pltpu.VMEM((width, SPAN), bf16),
            pltpu.VMEM((width, SPAN), f32),
            pltpu.VMEM((width, SPAN), f32),
            pltpu.VMEM((width, state), f32),
            pltpu.VMEM((CHUNKS, chunk, state), bf16),
            pltpu.VMEM((CHUNKS, chunk, state), bf16),
            pltpu.VMEM((CHUNKS, chunk, SPAN), bf16),
            pltpu.VMEM((n, rows, SPAN), bf16),
            pltpu.VMEM((n, 8, LANES), f32),
            pltpu.VMEM((8, LANES), f32),
            square,
            square,
            square,
            square,
            square,
            pltpu.VMEM((CHUNKS, SPAN, LANES), f32),
            square,
            pltpu.VMEM((SPAN, state), bf16),
            pltpu.VMEM((SPAN, state), bf16),
            pltpu.VMEM((8, LANES), f32),
            pltpu.VMEM((rows, LANES), f32),
            dma((7,)),
            dma((3,)),
            dma((3,)),
            dma((CHUNKS,)),
            dma((CHUNKS,)),
            dma((n,)),
            dma((n,)),
            dma((n,)),
            dma((n,)),
        ],
        compiler_params=pltpu.CompilerParams(
            collective_id=0, has_side_effects=True, vmem_limit_bytes=56 * 1024 * 1024
        ),
        cost_estimate=pl.CostEstimate(
            flops=8 * SPAN * SPAN * width, bytes_accessed=6 * SPAN * width, transcendentals=0
        ),
    )(
        x_in,
        z_in,
        b_in,
        c_in,
        dt_raw.T,
        dt_bias[None, :],
        a_log[None, :],
        d_skip[None, :],
        conv_x,
        conv_b,
        conv_c,
        gain,
    )


def solution(mesh):
    return jax.shard_map(
        shards,
        mesh=mesh,
        in_specs=(
            P("ctx", "tp"),
            P("ctx", "tp"),
            P("ctx", "tp"),
            P("ctx", "tp"),
            P("ctx", "tp"),
            P("tp"),
            P("tp"),
            P("tp"),
            P(None, "tp"),
            P(None, "tp"),
            P(None, "tp"),
            P("tp"),
        ),
        out_specs=P(("tp", "ctx"), None),
        check_vma=False,
    )
```

```python
import functools

import jax
import jax.numpy as jnp
from jax import lax
from jax.experimental import pallas as pl
from jax.experimental.pallas import tpu as pltpu
from jax.sharding import PartitionSpec as P

SPAN = 128
LANES = 128
HALO = 16
CHUNKS = 8
EPS = 1e-05
LOG2E = 1.4426950408889634
MESH = pl.DeviceIdType.MESH


def silu(value):
    half = 0.5 * value
    return half + half * jnp.tanh(half)


def conv_silu(pad, taps, count):
    total = taps[0:1] * pad[8 - count + 1 : 8 - count + 1 + SPAN, :]
    for tap in range(1, count):
        start = 8 - count + 1 + tap
        total = total + taps[tap : tap + 1] * pad[start : start + SPAN, :]
    return silu(total).astype(jnp.bfloat16)


def kernel(
    n,
    x_ref,
    z_ref,
    b_ref,
    c_ref,
    dt_ref,
    bias_ref,
    alog_ref,
    skip_ref,
    cx_ref,
    cb_ref,
    cc_ref,
    recv,
    scale_in,
    x_buf,
    z_buf,
    b_buf,
    c_buf,
    cx_buf,
    cb_buf,
    cc_buf,
    halo_x,
    halo_b,
    halo_c,
    small,
    pad,
    x_t,
    z_t,
    pre,
    upd,
    state_in,
    state_out,
    stage,
    scale_out,
    log_rows,
    mix_rows,
    grow_rows,
    last_rows,
    skip_rows,
    cols,
    scores,
    b_act,
    c_act,
    ssq,
    above,
    load,
    halo_send,
    halo_recv,
    state_send,
    state_recv,
    out_send,
    out_recv,
    scale_send,
    scale_recv,
):
    width = x_ref.shape[1]
    heads = dt_ref.shape[0]
    head = width // heads
    per_block = LANES // head
    chunk = width // CHUNKS
    blocks = chunk // LANES
    chunk_heads = heads // CHUNKS
    rows = width // n
    parts = chunk // rows
    taps = cx_ref.shape[0]
    me = lax.axis_index("ctx")
    nxt = lax.rem(me + 1, n)

    barrier = pltpu.get_barrier_semaphore()

    def greet(other):
        pl.semaphore_signal(barrier, inc=1, device_id={"ctx": other}, device_id_type=MESH)

    @pl.when(me > 0)
    def _():
        greet(me - 1)

    @pl.when(me < n - 1)
    def _():
        greet(me + 1)

    def tell_above():
        pl.semaphore_signal(above, inc=1, device_id={"ctx": me - 1}, device_id_type=MESH)

    def pass_above():
        pl.semaphore_wait(above, 1)

        @pl.when(me > 0)
        def _():
            tell_above()

    def halo_copy(index):
        source = (x_ref, b_ref, c_ref)[index]
        target = (halo_x, halo_b, halo_c)[index]
        return pltpu.make_async_remote_copy(
            src_ref=source.at[pl.ds(SPAN - HALO, HALO), :],
            dst_ref=target,
            send_sem=halo_send.at[index],
            recv_sem=halo_recv.at[index],
            device_id={"ctx": nxt},
            device_id_type=MESH,
        )

    pieces = min(2, blocks)
    piece = chunk // pieces

    def state_copy(k, p):
        return pltpu.make_async_remote_copy(
            src_ref=state_out.at[k, pl.ds(p * piece, piece), :],
            dst_ref=state_in.at[k, pl.ds(p * piece, piece), :],
            send_sem=state_send.at[k, p],
            recv_sem=state_recv.at[k, p],
            device_id={"ctx": nxt},
            device_id_type=MESH,
        )

    def out_copy(k, part, dest, slot):
        return pltpu.make_async_remote_copy(
            src_ref=stage.at[k, pl.ds(part * rows, rows), :],
            dst_ref=recv.at[slot],
            send_sem=out_send.at[dest],
            recv_sem=out_recv.at[slot],
            device_id={"ctx": dest},
            device_id_type=MESH,
        )

    def own_out(k, part):
        return pltpu.make_async_copy(
            stage.at[k, pl.ds(part * rows, rows), :], recv.at[me], out_recv.at[me]
        )

    def own_scale():
        return pltpu.make_async_copy(scale_out, scale_in.at[me], scale_recv.at[me])

    def scale_copy(dest, slot):
        return pltpu.make_async_remote_copy(
            src_ref=scale_out,
            dst_ref=scale_in.at[slot],
            send_sem=scale_send.at[dest],
            recv_sem=scale_recv.at[slot],
            device_id={"ctx": dest},
            device_id_type=MESH,
        )

    def loading(index):
        source = (x_ref, b_ref, c_ref, cx_ref, cb_ref, cc_ref, z_ref)[index]
        target = (x_buf, b_buf, c_buf, cx_buf, cb_buf, cc_buf, z_buf)[index]
        return pltpu.make_async_copy(source, target, load.at[index])

    for index in range(7):
        loading(index).start()

    def down_columns(row, count):
        return jnp.broadcast_to(row, (SPAN, count)).T

    small[...] = jnp.zeros_like(small)
    small[SPAN : SPAN + 1, 0:heads] = bias_ref[...]
    small[SPAN + 8 : SPAN + 9, 0:heads] = alog_ref[...]
    small[SPAN + 16 : SPAN + 17, 0:heads] = skip_ref[...]
    small[0:heads, :] = dt_ref[...]
    raw = small[0:SPAN, :] + down_columns(small[SPAN : SPAN + 1, :], LANES)
    delta = jnp.maximum(raw, 0.0) + jnp.log1p(jnp.exp(-jnp.abs(raw)))
    rate = -down_columns(jnp.exp(small[SPAN + 8 : SPAN + 9, :]), LANES) * delta
    down = lax.broadcasted_iota(jnp.int32, (SPAN, SPAN), 0)
    across = lax.broadcasted_iota(jnp.int32, (SPAN, SPAN), 1)
    upper = jnp.where(down <= across, 1.0, 0.0)
    logs = jnp.dot(
        rate, upper, precision=lax.Precision.HIGHEST, preferred_element_type=jnp.float32
    )
    last = jnp.broadcast_to(logs[:, SPAN - 1 : SPAN], (SPAN, LANES))
    log_rows[...] = logs * LOG2E
    grow_rows[...] = jnp.exp(logs)
    mix_rows[...] = jnp.exp(last - logs) * delta
    last_rows[...] = jnp.exp(last)
    skip_rows[...] = down_columns(small[SPAN + 16 : SPAN + 17, :], LANES)
    shifted = ((logs - jnp.log(delta)) * LOG2E).T
    for k in range(CHUNKS):
        cols[k, :, 0:chunk_heads] = shifted[:, k * chunk_heads : (k + 1) * chunk_heads]
    ssq[...] = jnp.zeros_like(ssq)

    ends = (me == 0) | (me == n - 1)

    @pl.when(ends)
    def _():
        pl.semaphore_wait(barrier, 1)

    @pl.when(jnp.logical_not(ends))
    def _():
        pl.semaphore_wait(barrier, 2)

    @pl.when(me == n - 1)
    def _():
        tell_above()

    @pl.when(me < n - 1)
    def _():
        for index in range(3):
            halo_copy(index).start()

    for index in range(6):
        loading(index).wait()

    @pl.when(me > 0)
    def _():
        for index in range(3):
            halo_copy(index).wait_recv()

    @pl.when(me == 0)
    def _():
        halo_x[...] = jnp.zeros_like(halo_x)
        halo_b[...] = jnp.zeros_like(halo_b)
        halo_c[...] = jnp.zeros_like(halo_c)
        state_in[...] = jnp.zeros_like(state_in)

    for index, (source, halo, weights, target) in enumerate(
        ((b_buf, halo_b, cb_buf, b_act), (c_buf, halo_c, cc_buf, c_act))
    ):
        pad[index, 0:8, :] = halo[...].astype(jnp.float32)[HALO - 8 :]
        pad[index, 8 : 8 + SPAN, :] = source[...].astype(jnp.float32)
        target[...] = conv_silu(pad.at[index], weights[...], taps)
    overlap = lax.dot_general(
        b_act[...], c_act[...], (((1,), (1,)), ((), ())), preferred_element_type=jnp.float32
    )
    scores[...] = jnp.where(down <= across, overlap, 0.0)

    def head_row(ref, index):
        return jnp.broadcast_to(ref[pl.ds(index, 1), :], (head, LANES))

    def block_rows(ref, k, j):
        first = k * chunk_heads + j * per_block
        return jnp.concatenate([head_row(ref, first + i) for i in range(per_block)], axis=0)

    def block_place(k, j):
        return pl.ds(pl.multiple_of(k * chunk + j * LANES, LANES), LANES)

    early = me < n // 2

    def chain(k):
        for p in range(pieces):

            @pl.when(me > 0)
            def _():
                state_copy(k, p).wait_recv()

            @pl.when(me < n - 1)
            def _():
                for j in range(p * piece // LANES, (p + 1) * piece // LANES):
                    entering = state_in[k, j * LANES : (j + 1) * LANES, :].astype(jnp.float32)
                    leaving = block_rows(last_rows, k, j) * entering + upd[block_place(k, j), :]
                    state_out[k, j * LANES : (j + 1) * LANES, :] = leaving.astype(jnp.bfloat16)
                state_copy(k, p).start()

    def updates(k, carry):
        for j in range(blocks):
            place = block_place(k, j)
            pad[j, 0:8, :] = halo_x[:, place].astype(jnp.float32)[HALO - 8 :]
            pad[j, 8 : 8 + SPAN, :] = x_buf[:, place].astype(jnp.float32)
            act = conv_silu(pad.at[j], cx_buf[:, place], taps)
            turned = act.T
            x_t[place, :] = turned
            scaled = (turned.astype(jnp.float32) * block_rows(mix_rows, k, j)).astype(jnp.bfloat16)
            upd[place, :] = jnp.dot(scaled, b_act[...], preferred_element_type=jnp.float32)

        @pl.when(early & (me > 0) & (k == jnp.minimum(2 * (n // 2 - 1 - me), CHUNKS - 1)))
        def _():
            pass_above()

        @pl.when(early)
        def _():
            chain(k)

        return carry

    @pl.when(jnp.logical_not(early) & (me < n - 1))
    def _():
        pass_above()

    lax.fori_loop(0, CHUNKS, updates, 0)

    @pl.when(me == 0)
    def _():
        pass_above()

    loading(6).wait()

    def within(k):
        shifts = cols[k]
        for j in range(blocks):
            place = block_place(k, j)
            z_t[place, :] = silu(z_buf[:, place].T.astype(jnp.float32))
            x_block = x_t[place, :]
            inner = []
            for i in range(per_block):
                which = j * per_block + i
                gap = (
                    log_rows[pl.ds(k * chunk_heads + which, 1), :] - shifts[:, which : which + 1]
                )
                weights = (scores[...] * jnp.exp2(gap)).astype(jnp.bfloat16)
                inner.append(
                    jnp.dot(
                        x_block[i * head : (i + 1) * head],
                        weights,
                        preferred_element_type=jnp.float32,
                    )
                )
            pre[place, :] = jnp.concatenate(inner, axis=0) + block_rows(
                skip_rows, k, j
            ) * x_block.astype(jnp.float32)

    ahead = jnp.where(early, 0, jnp.minimum(2 * (me - n // 2) + 2, CHUNKS))

    def within_ahead(k, carry):
        within(k)
        return carry

    lax.fori_loop(0, ahead, within_ahead, 0)

    def outputs(k, carry):
        @pl.when(k >= ahead)
        def _():
            within(k)

        @pl.when(jnp.logical_not(early))
        def _():
            chain(k)

        squares = ssq[0:1, :]
        for j in range(blocks):
            place = block_place(k, j)
            outer = lax.dot_general(
                state_in[k, j * LANES : (j + 1) * LANES, :],
                c_act[...],
                (((1,), (1,)), ((), ())),
                preferred_element_type=jnp.float32,
            )
            gated = (pre[place, :] + block_rows(grow_rows, k, j) * outer) * z_t[place, :]
            squares = squares + jnp.sum(gated * gated, axis=0, keepdims=True)
            stage[k, j * LANES : (j + 1) * LANES, :] = gated.astype(jnp.bfloat16)
        ssq[0:1, :] = squares

        for part in range(parts):
            dest = k * parts + part

            @pl.when(dest != me)
            def _():
                out_copy(k, part, dest, me).start()

            @pl.when(dest == me)
            def _():
                own_out(k, part).start()

        return carry

    lax.fori_loop(0, CHUNKS, outputs, 0)

    scale = jnp.broadcast_to(lax.rsqrt(ssq[0:1, :] / width + EPS), (8, LANES))
    scale_out[...] = scale
    own_scale().start()

    def tell(other, carry):
        @pl.when(other != me)
        def _():
            scale_copy(other, me).start()

        return carry

    lax.fori_loop(0, n, tell, 0)

    def finish(source, carry):
        @pl.when(source != me)
        def _():
            out_copy(0, 0, source, source).wait_recv()
            scale_copy(source, source).wait_recv()

        @pl.when(source == me)
        def _():
            own_out(0, 0).wait()
            own_scale().wait()

        return carry

    lax.fori_loop(0, n, finish, 0)

    @pl.when(me < n - 1)
    def _():
        for index in range(3):
            halo_copy(index).wait_send()

        def drain_state(k, carry):
            for p in range(pieces):
                state_copy(k, p).wait_send()
            return carry

        lax.fori_loop(0, CHUNKS, drain_state, 0)

    def drain(other, carry):
        @pl.when(other != me)
        def _():
            out_copy(0, 0, other, me).wait_send()
            scale_copy(other, me).wait_send()

        return carry

    lax.fori_loop(0, n, drain, 0)


def normalise(gated_ref, scale_ref, gain_ref, out_ref, gain_col):
    rows = out_ref.shape[0]
    me = lax.axis_index("ctx")

    @pl.when(pl.program_id(0) == 0)
    def _():
        if rows % LANES == 0:
            own = gain_ref[:, pl.ds(pl.multiple_of(me * rows, LANES), rows)]
        else:
            own = gain_ref[pl.ds(me, 1), :]
        gain_col[...] = jnp.broadcast_to(own, (LANES, rows)).T

    for i in range(gated_ref.shape[0]):
        value = gated_ref[i].astype(jnp.float32) * scale_ref[i, 0:1, :] * gain_col[...]
        out_ref[:, i * SPAN : (i + 1) * SPAN] = value.astype(jnp.bfloat16)


def shards(
    x_in, z_in, b_in, c_in, dt_raw, dt_bias, a_log, d_skip, conv_x, conv_b, conv_c, norm_gain
):
    n = lax.axis_size("ctx")
    width = x_in.shape[1]
    state = b_in.shape[1]
    rows = width // n
    chunk = width // CHUNKS
    gain = norm_gain.reshape((1, width) if rows % LANES == 0 else (n, rows))
    taps = conv_x.shape[0]
    hbm = pl.BlockSpec(memory_space=pl.ANY)
    vmem = pl.BlockSpec(memory_space=pltpu.VMEM)
    f32, bf16 = jnp.float32, jnp.bfloat16
    dma = pltpu.SemaphoreType.DMA
    square = pltpu.VMEM((LANES, LANES), f32)
    gated, scales = pl.pallas_call(
        functools.partial(kernel, n),
        out_shape=(
            jax.ShapeDtypeStruct((n, rows, SPAN), bf16),
            jax.ShapeDtypeStruct((n, 8, LANES), f32),
        ),
        in_specs=[hbm] * 4 + [vmem] * 4 + [hbm] * 3,
        out_specs=(hbm, hbm),
        scratch_shapes=[
            pltpu.VMEM((SPAN, width), bf16),
            pltpu.VMEM((SPAN, width), bf16),
            pltpu.VMEM((SPAN, state), bf16),
            pltpu.VMEM((SPAN, state), bf16),
            pltpu.VMEM((taps, width), f32),
            pltpu.VMEM((taps, state), f32),
            pltpu.VMEM((taps, state), f32),
            pltpu.VMEM((HALO, width), bf16),
            pltpu.VMEM((HALO, state), bf16),
            pltpu.VMEM((HALO, state), bf16),
            pltpu.VMEM((SPAN + 24, LANES), f32),
            pltpu.VMEM((max(2, chunk // LANES), SPAN + 8, LANES), f32),
            pltpu.VMEM((width, SPAN), bf16),
            pltpu.VMEM((width, SPAN), f32),
            pltpu.VMEM((width, SPAN), f32),
            pltpu.VMEM((width, state), f32),
            pltpu.VMEM((CHUNKS, chunk, state), bf16),
            pltpu.VMEM((CHUNKS, chunk, state), bf16),
            pltpu.VMEM((CHUNKS, chunk, SPAN), bf16),
            pltpu.VMEM((8, LANES), f32),
            square,
            square,
            square,
            square,
            square,
            pltpu.VMEM((CHUNKS, SPAN, LANES), f32),
            square,
            pltpu.VMEM((SPAN, state), bf16),
            pltpu.VMEM((SPAN, state), bf16),
            pltpu.VMEM((8, LANES), f32),
            pltpu.SemaphoreType.REGULAR,
            dma((7,)),
            dma((3,)),
            dma((3,)),
            dma((CHUNKS, 2)),
            dma((CHUNKS, 2)),
            dma((n,)),
            dma((n,)),
            dma((n,)),
            dma((n,)),
        ],
        compiler_params=pltpu.CompilerParams(
            collective_id=0, has_side_effects=True, vmem_limit_bytes=56 * 1024 * 1024
        ),
        cost_estimate=pl.CostEstimate(
            flops=8 * SPAN * SPAN * width, bytes_accessed=6 * SPAN * width, transcendentals=0
        ),
    )(
        x_in,
        z_in,
        b_in,
        c_in,
        dt_raw.T,
        dt_bias[None, :],
        a_log[None, :],
        d_skip[None, :],
        conv_x,
        conv_b,
        conv_c,
    )
    return pl.pallas_call(
        normalise,
        grid=(2,),
        out_shape=jax.ShapeDtypeStruct((rows, n * SPAN), bf16),
        in_specs=[
            pl.BlockSpec((n // 2, rows, SPAN), lambda i: (i, 0, 0)),
            pl.BlockSpec((n // 2, 8, LANES), lambda i: (i, 0, 0)),
            pl.BlockSpec(gain.shape, lambda i: (0, 0)),
        ],
        out_specs=pl.BlockSpec((rows, n // 2 * SPAN), lambda i: (0, i)),
        scratch_shapes=[pltpu.VMEM((rows, LANES), f32)],
        compiler_params=pltpu.CompilerParams(vmem_limit_bytes=56 * 1024 * 1024),
    )(gated, scales, gain)


def solution(mesh):
    return jax.shard_map(
        shards,
        mesh=mesh,
        in_specs=(
            P("ctx", "tp"),
            P("ctx", "tp"),
            P("ctx", "tp"),
            P("ctx", "tp"),
            P("ctx", "tp"),
            P("tp"),
            P("tp"),
            P("tp"),
            P(None, "tp"),
            P(None, "tp"),
            P(None, "tp"),
            P("tp"),
        ),
        out_specs=P(("tp", "ctx"), None),
        check_vma=False,
    )
```

```python
import functools

import jax
import jax.numpy as jnp
from jax import lax
from jax.experimental import pallas as pl
from jax.experimental.pallas import tpu as pltpu
from jax.sharding import PartitionSpec as P

SPAN = 128
LANES = 128
HALO = 16
CHUNKS = 8
EPS = 1e-05
LOG2E = 1.4426950408889634
MESH = pl.DeviceIdType.MESH


def silu(value):
    half = 0.5 * value
    return half + half * jnp.tanh(half)


def conv_silu(pad, taps, count):
    total = taps[0:1] * pad[8 - count + 1 : 8 - count + 1 + SPAN, :]
    for tap in range(1, count):
        start = 8 - count + 1 + tap
        total = total + taps[tap : tap + 1] * pad[start : start + SPAN, :]
    return silu(total).astype(jnp.bfloat16)


def kernel(
    n,
    x_ref,
    z_ref,
    b_ref,
    c_ref,
    dt_ref,
    bias_ref,
    alog_ref,
    skip_ref,
    cx_ref,
    cb_ref,
    cc_ref,
    recv,
    scale_in,
    x_buf,
    z_buf,
    b_buf,
    c_buf,
    cx_buf,
    cb_buf,
    cc_buf,
    halo_x,
    halo_b,
    halo_c,
    small,
    pad,
    x_t,
    z_t,
    pre,
    upd,
    state_in,
    state_out,
    stage,
    scale_out,
    log_rows,
    mix_rows,
    grow_rows,
    last_rows,
    skip_rows,
    cols,
    turned_cols,
    scores,
    b_act,
    c_act,
    ssq,
    above,
    load,
    halo_send,
    halo_recv,
    state_send,
    state_recv,
    out_send,
    out_recv,
    scale_send,
    scale_recv,
):
    width = x_ref.shape[1]
    heads = dt_ref.shape[0]
    head = width // heads
    per_block = LANES // head
    chunk = width // CHUNKS
    blocks = chunk // LANES
    chunk_heads = heads // CHUNKS
    rows = width // n
    parts = chunk // rows
    taps = cx_ref.shape[0]
    me = lax.axis_index("ctx")
    nxt = lax.rem(me + 1, n)

    barrier = pltpu.get_barrier_semaphore()

    def greet(other):
        pl.semaphore_signal(barrier, inc=1, device_id={"ctx": other}, device_id_type=MESH)

    @pl.when(me > 0)
    def _():
        greet(me - 1)

    @pl.when(me < n - 1)
    def _():
        greet(me + 1)

    def tell_above():
        pl.semaphore_signal(above, inc=1, device_id={"ctx": me - 1}, device_id_type=MESH)

    def pass_above():
        pl.semaphore_wait(above, 1)

        @pl.when(me > 0)
        def _():
            tell_above()

    def halo_copy(index):
        source = (b_ref, c_ref)[index]
        target = (halo_b, halo_c)[index]
        return pltpu.make_async_remote_copy(
            src_ref=source.at[pl.ds(SPAN - HALO, HALO), :],
            dst_ref=target,
            send_sem=halo_send.at[CHUNKS + index],
            recv_sem=halo_recv.at[CHUNKS + index],
            device_id={"ctx": nxt},
            device_id_type=MESH,
        )

    def halo_x_copy(k):
        place = pl.ds(pl.multiple_of(k * chunk, LANES), chunk)
        return pltpu.make_async_remote_copy(
            src_ref=x_ref.at[pl.ds(SPAN - HALO, HALO), place],
            dst_ref=halo_x.at[:, place],
            send_sem=halo_send.at[k],
            recv_sem=halo_recv.at[k],
            device_id={"ctx": nxt},
            device_id_type=MESH,
        )

    pieces = min(2, blocks)
    piece = chunk // pieces

    def state_copy(k, p):
        return pltpu.make_async_remote_copy(
            src_ref=state_out.at[k, pl.ds(p * piece, piece), :],
            dst_ref=state_in.at[k, pl.ds(p * piece, piece), :],
            send_sem=state_send.at[k, p],
            recv_sem=state_recv.at[k, p],
            device_id={"ctx": nxt},
            device_id_type=MESH,
        )

    def out_copy(k, part, dest, slot):
        return pltpu.make_async_remote_copy(
            src_ref=stage.at[k, pl.ds(part * rows, rows), :],
            dst_ref=recv.at[slot],
            send_sem=out_send.at[dest],
            recv_sem=out_recv.at[slot],
            device_id={"ctx": dest},
            device_id_type=MESH,
        )

    def own_out(k, part):
        return pltpu.make_async_copy(
            stage.at[k, pl.ds(part * rows, rows), :], recv.at[me], out_recv.at[me]
        )

    def own_scale():
        return pltpu.make_async_copy(scale_out, scale_in.at[me], scale_recv.at[me])

    def scale_copy(dest, slot):
        return pltpu.make_async_remote_copy(
            src_ref=scale_out,
            dst_ref=scale_in.at[slot],
            send_sem=scale_send.at[dest],
            recv_sem=scale_recv.at[slot],
            device_id={"ctx": dest},
            device_id_type=MESH,
        )

    def loading(index):
        source = (x_ref, b_ref, c_ref, cx_ref, cb_ref, cc_ref, z_ref)[index]
        target = (x_buf, b_buf, c_buf, cx_buf, cb_buf, cc_buf, z_buf)[index]
        return pltpu.make_async_copy(source, target, load.at[index])

    for index in range(7):
        loading(index).start()

    def down_columns(row, count):
        return jnp.broadcast_to(row, (SPAN, count)).T

    small[...] = jnp.zeros_like(small)
    small[SPAN : SPAN + 1, 0:heads] = bias_ref[...]
    small[SPAN + 8 : SPAN + 9, 0:heads] = alog_ref[...]
    small[SPAN + 16 : SPAN + 17, 0:heads] = skip_ref[...]
    small[0:heads, :] = dt_ref[...]
    raw = small[0:SPAN, :] + down_columns(small[SPAN : SPAN + 1, :], LANES)
    delta = jnp.maximum(raw, 0.0) + jnp.log1p(jnp.exp(-jnp.abs(raw)))
    rate = -down_columns(jnp.exp(small[SPAN + 8 : SPAN + 9, :]), LANES) * delta
    down = lax.broadcasted_iota(jnp.int32, (SPAN, SPAN), 0)
    across = lax.broadcasted_iota(jnp.int32, (SPAN, SPAN), 1)
    upper = jnp.where(down <= across, 1.0, 0.0)
    logs = jnp.dot(
        rate, upper, precision=lax.Precision.HIGHEST, preferred_element_type=jnp.float32
    )
    last = jnp.broadcast_to(logs[:, SPAN - 1 : SPAN], (SPAN, LANES))
    log_rows[...] = logs * LOG2E
    mix_rows[...] = jnp.exp(last - logs) * delta
    last_rows[...] = jnp.exp(last)
    turned_cols[...] = (logs - jnp.log(delta)) * LOG2E

    ends = (me == 0) | (me == n - 1)

    @pl.when(ends)
    def _():
        pl.semaphore_wait(barrier, 1)

    @pl.when(jnp.logical_not(ends))
    def _():
        pl.semaphore_wait(barrier, 2)

    @pl.when(me == n - 1)
    def _():
        tell_above()

    @pl.when(me < n - 1)
    def _():
        halo_copy(0).start()
        for k in range(CHUNKS):
            halo_x_copy(k).start()
        halo_copy(1).start()

    early = me < n // 2

    @pl.when(jnp.logical_not(early) & (me < n - 1))
    def _():
        pass_above()

    for index in range(6):
        loading(index).wait()

    @pl.when(me > 0)
    def _():
        halo_copy(0).wait_recv()

    @pl.when(me == 0)
    def _():
        halo_x[...] = jnp.zeros_like(halo_x)
        halo_b[...] = jnp.zeros_like(halo_b)
        halo_c[...] = jnp.zeros_like(halo_c)
        state_in[...] = jnp.zeros_like(state_in)

    def project(slot, source, halo, weights, target):
        pad[slot, 0:8, :] = halo[...].astype(jnp.float32)[HALO - 8 :]
        pad[slot, 8 : 8 + SPAN, :] = source[...].astype(jnp.float32)
        target[...] = conv_silu(pad.at[slot], weights[...], taps)

    project(0, b_buf, halo_b, cb_buf, b_act)

    def head_row(ref, index):
        return jnp.broadcast_to(ref[pl.ds(index, 1), :], (head, LANES))

    def block_rows(ref, k, j):
        first = k * chunk_heads + j * per_block
        return jnp.concatenate([head_row(ref, first + i) for i in range(per_block)], axis=0)

    def block_place(k, j):
        return pl.ds(pl.multiple_of(k * chunk + j * LANES, LANES), LANES)

    def chain(k):
        for p in range(pieces):

            @pl.when(me > 0)
            def _():
                state_copy(k, p).wait_recv()

            @pl.when(me < n - 1)
            def _():
                for j in range(p * piece // LANES, (p + 1) * piece // LANES):
                    entering = state_in[k, j * LANES : (j + 1) * LANES, :].astype(jnp.float32)
                    leaving = block_rows(last_rows, k, j) * entering + upd[block_place(k, j), :]
                    state_out[k, j * LANES : (j + 1) * LANES, :] = leaving.astype(jnp.bfloat16)
                state_copy(k, p).start()

    def updates(k, carry):
        @pl.when(me > 0)
        def _():
            halo_x_copy(k).wait_recv()

        for j in range(blocks):
            place = block_place(k, j)
            pad[j, 0:8, :] = halo_x[:, place].astype(jnp.float32)[HALO - 8 :]
            pad[j, 8 : 8 + SPAN, :] = x_buf[:, place].astype(jnp.float32)
            act = conv_silu(pad.at[j], cx_buf[:, place], taps)
            turned = act.T
            x_t[place, :] = turned
            scaled = (turned.astype(jnp.float32) * block_rows(mix_rows, k, j)).astype(jnp.bfloat16)
            upd[place, :] = jnp.dot(scaled, b_act[...], preferred_element_type=jnp.float32)

        @pl.when(early & (me > 0) & (k == jnp.minimum(2 * (n // 2 - 1 - me) + 1, CHUNKS - 1)))
        def _():
            pass_above()

        @pl.when(early)
        def _():
            chain(k)

        return carry

    lax.fori_loop(0, CHUNKS, updates, 0)

    @pl.when(me > 0)
    def _():
        halo_copy(1).wait_recv()

    project(1, c_buf, halo_c, cc_buf, c_act)
    overlap = lax.dot_general(
        b_act[...], c_act[...], (((1,), (1,)), ((), ())), preferred_element_type=jnp.float32
    )
    scores[...] = jnp.where(down <= across, overlap, 0.0)
    grow_rows[...] = jnp.exp2(log_rows[...])
    skip_rows[...] = down_columns(small[SPAN + 16 : SPAN + 17, :], LANES)
    shifted = turned_cols[...].T
    for k in range(CHUNKS):
        cols[k, :, 0:chunk_heads] = shifted[:, k * chunk_heads : (k + 1) * chunk_heads]
    ssq[...] = jnp.zeros_like(ssq)
    loading(6).wait()

    def within(k):
        shifts = cols[k]
        for j in range(blocks):
            place = block_place(k, j)
            z_t[place, :] = silu(z_buf[:, place].T.astype(jnp.float32))
            x_block = x_t[place, :]
            inner = []
            for i in range(per_block):
                which = j * per_block + i
                gap = (
                    log_rows[pl.ds(k * chunk_heads + which, 1), :] - shifts[:, which : which + 1]
                )
                weights = (scores[...] * jnp.exp2(gap)).astype(jnp.bfloat16)
                inner.append(
                    jnp.dot(
                        x_block[i * head : (i + 1) * head],
                        weights,
                        preferred_element_type=jnp.float32,
                    )
                )
            pre[place, :] = jnp.concatenate(inner, axis=0) + block_rows(
                skip_rows, k, j
            ) * x_block.astype(jnp.float32)

    ahead = jnp.where(early, 0, jnp.minimum(2 * (me - n // 2) + 2, CHUNKS))
    ahead = jnp.where(me == 0, CHUNKS // 2, ahead)

    def within_ahead(k, carry):
        within(k)
        return carry

    lax.fori_loop(0, ahead, within_ahead, 0)

    @pl.when(me == 0)
    def _():
        pass_above()

    def outputs(k, carry):
        @pl.when(k >= ahead)
        def _():
            within(k)

        @pl.when(jnp.logical_not(early))
        def _():
            chain(k)

        squares = ssq[0:1, :]
        for j in range(blocks):
            place = block_place(k, j)
            outer = lax.dot_general(
                state_in[k, j * LANES : (j + 1) * LANES, :],
                c_act[...],
                (((1,), (1,)), ((), ())),
                preferred_element_type=jnp.float32,
            )
            gated = (pre[place, :] + block_rows(grow_rows, k, j) * outer) * z_t[place, :]
            squares = squares + jnp.sum(gated * gated, axis=0, keepdims=True)
            stage[k, j * LANES : (j + 1) * LANES, :] = gated.astype(jnp.bfloat16)
        ssq[0:1, :] = squares

        for part in range(parts):
            dest = k * parts + part

            @pl.when(dest != me)
            def _():
                out_copy(k, part, dest, me).start()

            @pl.when(dest == me)
            def _():
                own_out(k, part).start()

        return carry

    lax.fori_loop(0, CHUNKS, outputs, 0)

    scale = jnp.broadcast_to(lax.rsqrt(ssq[0:1, :] / width + EPS), (8, LANES))
    scale_out[...] = scale
    own_scale().start()

    def tell(other, carry):
        @pl.when(other != me)
        def _():
            scale_copy(other, me).start()

        return carry

    lax.fori_loop(0, n, tell, 0)

    def finish(source, carry):
        @pl.when(source != me)
        def _():
            out_copy(0, 0, source, source).wait_recv()
            scale_copy(source, source).wait_recv()

        @pl.when(source == me)
        def _():
            own_out(0, 0).wait()
            own_scale().wait()

        return carry

    lax.fori_loop(0, n, finish, 0)

    @pl.when(me < n - 1)
    def _():
        for index in range(2):
            halo_copy(index).wait_send()

        def drain_state(k, carry):
            halo_x_copy(k).wait_send()
            for p in range(pieces):
                state_copy(k, p).wait_send()
            return carry

        lax.fori_loop(0, CHUNKS, drain_state, 0)

    def drain(other, carry):
        @pl.when(other != me)
        def _():
            out_copy(0, 0, other, me).wait_send()
            scale_copy(other, me).wait_send()

        return carry

    lax.fori_loop(0, n, drain, 0)


def normalise(rows, gated_ref, scale_ref, gain_ref, out_ref, gain_col):
    me = lax.axis_index("ctx")
    step = pl.program_id(0)
    share = out_ref.shape[0]

    @pl.when(step == 0)
    def _():
        if rows % LANES == 0:
            own = gain_ref[:, pl.ds(pl.multiple_of(me * rows, LANES), rows)]
        else:
            own = gain_ref[pl.ds(me, 1), :]
        gain_col[...] = jnp.broadcast_to(own, (LANES, rows)).T

    gain = gain_col[pl.ds(pl.multiple_of(step * share, share), share), :]
    for i in range(gated_ref.shape[0]):
        value = gated_ref[i].astype(jnp.float32) * scale_ref[i, 0:1, :] * gain
        out_ref[:, i * SPAN : (i + 1) * SPAN] = value.astype(jnp.bfloat16)


def shards(
    x_in, z_in, b_in, c_in, dt_raw, dt_bias, a_log, d_skip, conv_x, conv_b, conv_c, norm_gain
):
    n = lax.axis_size("ctx")
    width = x_in.shape[1]
    state = b_in.shape[1]
    rows = width // n
    chunk = width // CHUNKS
    gain = norm_gain.reshape((1, width) if rows % LANES == 0 else (n, rows))
    taps = conv_x.shape[0]
    hbm = pl.BlockSpec(memory_space=pl.ANY)
    vmem = pl.BlockSpec(memory_space=pltpu.VMEM)
    f32, bf16 = jnp.float32, jnp.bfloat16
    dma = pltpu.SemaphoreType.DMA
    square = pltpu.VMEM((LANES, LANES), f32)
    gated, scales = pl.pallas_call(
        functools.partial(kernel, n),
        out_shape=(
            jax.ShapeDtypeStruct((n, rows, SPAN), bf16),
            jax.ShapeDtypeStruct((n, 8, LANES), f32),
        ),
        in_specs=[hbm] * 4 + [vmem] * 4 + [hbm] * 3,
        out_specs=(hbm, hbm),
        scratch_shapes=[
            pltpu.VMEM((SPAN, width), bf16),
            pltpu.VMEM((SPAN, width), bf16),
            pltpu.VMEM((SPAN, state), bf16),
            pltpu.VMEM((SPAN, state), bf16),
            pltpu.VMEM((taps, width), f32),
            pltpu.VMEM((taps, state), f32),
            pltpu.VMEM((taps, state), f32),
            pltpu.VMEM((HALO, width), bf16),
            pltpu.VMEM((HALO, state), bf16),
            pltpu.VMEM((HALO, state), bf16),
            pltpu.VMEM((SPAN + 24, LANES), f32),
            pltpu.VMEM((max(2, chunk // LANES), SPAN + 8, LANES), f32),
            pltpu.VMEM((width, SPAN), bf16),
            pltpu.VMEM((width, SPAN), f32),
            pltpu.VMEM((width, SPAN), f32),
            pltpu.VMEM((width, state), f32),
            pltpu.VMEM((CHUNKS, chunk, state), bf16),
            pltpu.VMEM((CHUNKS, chunk, state), bf16),
            pltpu.VMEM((CHUNKS, chunk, SPAN), bf16),
            pltpu.VMEM((8, LANES), f32),
            square,
            square,
            square,
            square,
            square,
            pltpu.VMEM((CHUNKS, SPAN, LANES), f32),
            square,
            square,
            pltpu.VMEM((SPAN, state), bf16),
            pltpu.VMEM((SPAN, state), bf16),
            pltpu.VMEM((8, LANES), f32),
            pltpu.SemaphoreType.REGULAR,
            dma((7,)),
            dma((CHUNKS + 2,)),
            dma((CHUNKS + 2,)),
            dma((CHUNKS, 2)),
            dma((CHUNKS, 2)),
            dma((n,)),
            dma((n,)),
            dma((n,)),
            dma((n,)),
        ],
        compiler_params=pltpu.CompilerParams(
            collective_id=0, has_side_effects=True, vmem_limit_bytes=56 * 1024 * 1024
        ),
        cost_estimate=pl.CostEstimate(
            flops=8 * SPAN * SPAN * width, bytes_accessed=6 * SPAN * width, transcendentals=0
        ),
    )(
        x_in,
        z_in,
        b_in,
        c_in,
        dt_raw.T,
        dt_bias[None, :],
        a_log[None, :],
        d_skip[None, :],
        conv_x,
        conv_b,
        conv_c,
    )
    share = rows // 2 if rows % 256 == 0 else rows
    return pl.pallas_call(
        functools.partial(normalise, rows),
        grid=(rows // share,),
        out_shape=jax.ShapeDtypeStruct((rows, n * SPAN), bf16),
        in_specs=[
            pl.BlockSpec((n, share, SPAN), lambda i: (0, i, 0)),
            pl.BlockSpec((n, 8, LANES), lambda i: (0, 0, 0)),
            pl.BlockSpec(gain.shape, lambda i: (0, 0)),
        ],
        out_specs=pl.BlockSpec((share, n * SPAN), lambda i: (i, 0)),
        scratch_shapes=[pltpu.VMEM((rows, LANES), f32)],
        compiler_params=pltpu.CompilerParams(vmem_limit_bytes=56 * 1024 * 1024),
    )(gated, scales, gain)


def solution(mesh):
    return jax.shard_map(
        shards,
        mesh=mesh,
        in_specs=(
            P("ctx", "tp"),
            P("ctx", "tp"),
            P("ctx", "tp"),
            P("ctx", "tp"),
            P("ctx", "tp"),
            P("tp"),
            P("tp"),
            P("tp"),
            P(None, "tp"),
            P(None, "tp"),
            P(None, "tp"),
            P("tp"),
        ),
        out_specs=P(("tp", "ctx"), None),
        check_vma=False,
    )
```

```python
import functools

import jax
import jax.numpy as jnp
from jax import lax
from jax.experimental import pallas as pl
from jax.experimental.pallas import tpu as pltpu
from jax.sharding import PartitionSpec as P

SPAN = 128
LANES = 128
HALO = 16
CHUNKS = 8
EPS = 1e-05
LOG2E = 1.4426950408889634
MESH = pl.DeviceIdType.MESH


def silu(value):
    half = 0.5 * value
    return half + half * jnp.tanh(half)


def conv_silu(pad, taps, count):
    total = taps[0:1] * pad[8 - count + 1 : 8 - count + 1 + SPAN, :]
    for tap in range(1, count):
        start = 8 - count + 1 + tap
        total = total + taps[tap : tap + 1] * pad[start : start + SPAN, :]
    return silu(total).astype(jnp.bfloat16)


def kernel(
    n,
    x_ref,
    z_ref,
    b_ref,
    c_ref,
    dt_ref,
    bias_ref,
    alog_ref,
    skip_ref,
    cx_ref,
    cb_ref,
    cc_ref,
    recv,
    scale_in,
    x_buf,
    z_buf,
    b_buf,
    c_buf,
    cx_buf,
    cb_buf,
    cc_buf,
    halo_x,
    halo_b,
    halo_c,
    small,
    pad,
    x_t,
    z_t,
    pre,
    upd,
    state_in,
    state_out,
    stage,
    scale_out,
    log_rows,
    mix_rows,
    grow_rows,
    last_rows,
    skip_rows,
    cols,
    turned_cols,
    scores,
    b_act,
    c_act,
    ssq,
    above,
    load,
    halo_send,
    halo_recv,
    state_send,
    state_recv,
    out_send,
    out_recv,
    scale_send,
    scale_recv,
):
    width = x_ref.shape[1]
    heads = dt_ref.shape[0]
    head = width // heads
    per_block = LANES // head
    chunk = width // CHUNKS
    blocks = chunk // LANES
    chunk_heads = heads // CHUNKS
    rows = width // n
    parts = chunk // rows
    taps = cx_ref.shape[0]
    me = lax.axis_index("ctx")
    nxt = lax.rem(me + 1, n)

    barrier = pltpu.get_barrier_semaphore()

    def greet(other):
        pl.semaphore_signal(barrier, inc=1, device_id={"ctx": other}, device_id_type=MESH)

    @pl.when(me > 0)
    def _():
        greet(me - 1)

    @pl.when(me < n - 1)
    def _():
        greet(me + 1)

    def tell_above():
        pl.semaphore_signal(above, inc=1, device_id={"ctx": me - 1}, device_id_type=MESH)

    def pass_above():
        pl.semaphore_wait(above, 1)

        @pl.when(me > 0)
        def _():
            tell_above()

    def halo_copy(index):
        source = (b_ref, c_ref)[index]
        target = (halo_b, halo_c)[index]
        return pltpu.make_async_remote_copy(
            src_ref=source.at[pl.ds(SPAN - HALO, HALO), :],
            dst_ref=target,
            send_sem=halo_send.at[CHUNKS + index],
            recv_sem=halo_recv.at[CHUNKS + index],
            device_id={"ctx": nxt},
            device_id_type=MESH,
        )

    def halo_x_copy(k):
        place = pl.ds(pl.multiple_of(k * chunk, LANES), chunk)
        return pltpu.make_async_remote_copy(
            src_ref=x_ref.at[pl.ds(SPAN - HALO, HALO), place],
            dst_ref=halo_x.at[:, place],
            send_sem=halo_send.at[k],
            recv_sem=halo_recv.at[k],
            device_id={"ctx": nxt},
            device_id_type=MESH,
        )

    pieces = min(2, blocks)
    piece = chunk // pieces

    def state_copy(k, p):
        return pltpu.make_async_remote_copy(
            src_ref=state_out.at[k, pl.ds(p * piece, piece), :],
            dst_ref=state_in.at[k, pl.ds(p * piece, piece), :],
            send_sem=state_send.at[k, p],
            recv_sem=state_recv.at[k, p],
            device_id={"ctx": nxt},
            device_id_type=MESH,
        )

    def out_copy(k, part, dest, slot):
        return pltpu.make_async_remote_copy(
            src_ref=stage.at[k, pl.ds(part * rows, rows), :],
            dst_ref=recv.at[slot],
            send_sem=out_send.at[dest],
            recv_sem=out_recv.at[slot],
            device_id={"ctx": dest},
            device_id_type=MESH,
        )

    def own_out(k, part):
        return pltpu.make_async_copy(
            stage.at[k, pl.ds(part * rows, rows), :], recv.at[me], out_recv.at[me]
        )

    def own_scale():
        return pltpu.make_async_copy(scale_out, scale_in.at[me], scale_recv.at[me])

    def scale_copy(dest, slot):
        return pltpu.make_async_remote_copy(
            src_ref=scale_out,
            dst_ref=scale_in.at[slot],
            send_sem=scale_send.at[dest],
            recv_sem=scale_recv.at[slot],
            device_id={"ctx": dest},
            device_id_type=MESH,
        )

    def loading(index):
        source = (x_ref, b_ref, c_ref, cx_ref, cb_ref, cc_ref, z_ref)[index]
        target = (x_buf, b_buf, c_buf, cx_buf, cb_buf, cc_buf, z_buf)[index]
        return pltpu.make_async_copy(source, target, load.at[index])

    for index in range(7):
        loading(index).start()

    def down_columns(row, count):
        return jnp.broadcast_to(row, (SPAN, count)).T

    small[...] = jnp.zeros_like(small)
    small[SPAN : SPAN + 1, 0:heads] = bias_ref[...]
    small[SPAN + 8 : SPAN + 9, 0:heads] = alog_ref[...]
    small[SPAN + 16 : SPAN + 17, 0:heads] = skip_ref[...]
    small[0:heads, :] = dt_ref[...]
    raw = small[0:SPAN, :] + down_columns(small[SPAN : SPAN + 1, :], LANES)
    delta = jnp.maximum(raw, 0.0) + jnp.log1p(jnp.exp(-jnp.abs(raw)))
    rate = -down_columns(jnp.exp(small[SPAN + 8 : SPAN + 9, :]), LANES) * delta
    down = lax.broadcasted_iota(jnp.int32, (SPAN, SPAN), 0)
    across = lax.broadcasted_iota(jnp.int32, (SPAN, SPAN), 1)
    upper = jnp.where(down <= across, 1.0, 0.0)
    logs = jnp.dot(
        rate, upper, precision=lax.Precision.HIGHEST, preferred_element_type=jnp.float32
    )
    last = jnp.broadcast_to(logs[:, SPAN - 1 : SPAN], (SPAN, LANES))
    log_rows[...] = logs * LOG2E
    mix_rows[...] = jnp.exp(last - logs) * delta
    last_rows[...] = jnp.exp(last)
    turned_cols[...] = (logs - jnp.log(delta)) * LOG2E

    ends = (me == 0) | (me == n - 1)

    @pl.when(ends)
    def _():
        pl.semaphore_wait(barrier, 1)

    @pl.when(jnp.logical_not(ends))
    def _():
        pl.semaphore_wait(barrier, 2)

    @pl.when(me == n - 1)
    def _():
        tell_above()

    @pl.when(me < n - 1)
    def _():
        halo_copy(0).start()
        halo_x_copy(0).start()
        halo_copy(1).start()
        for k in range(1, CHUNKS):
            halo_x_copy(k).start()

    early = me < n // 2

    @pl.when(jnp.logical_not(early) & (me < n - 1))
    def _():
        pass_above()

    for index in range(6):
        loading(index).wait()

    @pl.when(me > 0)
    def _():
        halo_copy(0).wait_recv()

    @pl.when(me == 0)
    def _():
        halo_x[...] = jnp.zeros_like(halo_x)
        halo_b[...] = jnp.zeros_like(halo_b)
        halo_c[...] = jnp.zeros_like(halo_c)
        state_in[...] = jnp.zeros_like(state_in)

    def project(slot, source, halo, weights, target):
        pad[slot, 0:8, :] = halo[...].astype(jnp.float32)[HALO - 8 :]
        pad[slot, 8 : 8 + SPAN, :] = source[...].astype(jnp.float32)
        target[...] = conv_silu(pad.at[slot], weights[...], taps)

    project(0, b_buf, halo_b, cb_buf, b_act)

    def head_row(ref, index):
        return jnp.broadcast_to(ref[pl.ds(index, 1), :], (head, LANES))

    def block_rows(ref, k, j):
        first = k * chunk_heads + j * per_block
        return jnp.concatenate([head_row(ref, first + i) for i in range(per_block)], axis=0)

    def block_place(k, j):
        return pl.ds(pl.multiple_of(k * chunk + j * LANES, LANES), LANES)

    def chain(k):
        for p in range(pieces):

            @pl.when(me > 0)
            def _():
                state_copy(k, p).wait_recv()

            @pl.when(me < n - 1)
            def _():
                for j in range(p * piece // LANES, (p + 1) * piece // LANES):
                    entering = state_in[k, j * LANES : (j + 1) * LANES, :].astype(jnp.float32)
                    leaving = block_rows(last_rows, k, j) * entering + upd[block_place(k, j), :]
                    state_out[k, j * LANES : (j + 1) * LANES, :] = leaving.astype(jnp.bfloat16)
                state_copy(k, p).start()

    def set_up():
        @pl.when(me > 0)
        def _():
            halo_copy(1).wait_recv()

        project(1, c_buf, halo_c, cc_buf, c_act)
        overlap = lax.dot_general(
            b_act[...], c_act[...], (((1,), (1,)), ((), ())), preferred_element_type=jnp.float32
        )
        scores[...] = jnp.where(down <= across, overlap, 0.0)
        grow_rows[...] = jnp.exp2(log_rows[...])
        skip_rows[...] = down_columns(small[SPAN + 16 : SPAN + 17, :], LANES)
        shifted = turned_cols[...].T
        for k in range(CHUNKS):
            cols[k, :, 0:chunk_heads] = shifted[:, k * chunk_heads : (k + 1) * chunk_heads]
        ssq[...] = jnp.zeros_like(ssq)

    def within(k):
        shifts = cols[k]
        for j in range(blocks):
            place = block_place(k, j)
            z_t[place, :] = silu(z_buf[:, place].T.astype(jnp.float32))
            x_block = x_t[place, :]
            inner = []
            for i in range(per_block):
                which = j * per_block + i
                gap = (
                    log_rows[pl.ds(k * chunk_heads + which, 1), :] - shifts[:, which : which + 1]
                )
                weights = (scores[...] * jnp.exp2(gap)).astype(jnp.bfloat16)
                inner.append(
                    jnp.dot(
                        x_block[i * head : (i + 1) * head],
                        weights,
                        preferred_element_type=jnp.float32,
                    )
                )
            pre[place, :] = jnp.concatenate(inner, axis=0) + block_rows(
                skip_rows, k, j
            ) * x_block.astype(jnp.float32)

    far_first = early & (me > 0)
    lag = jnp.where(far_first, jnp.minimum(2 * (me - 1), CHUNKS), 0)

    def order(step):
        return jnp.where(far_first, lax.rem(step + CHUNKS // 2, CHUNKS), step)

    def updates(k):
        @pl.when(me > 0)
        def _():
            halo_x_copy(k).wait_recv()

        for j in range(blocks):
            place = block_place(k, j)
            pad[j, 0:8, :] = halo_x[:, place].astype(jnp.float32)[HALO - 8 :]
            pad[j, 8 : 8 + SPAN, :] = x_buf[:, place].astype(jnp.float32)
            act = conv_silu(pad.at[j], cx_buf[:, place], taps)
            turned = act.T
            x_t[place, :] = turned
            scaled = (turned.astype(jnp.float32) * block_rows(mix_rows, k, j)).astype(jnp.bfloat16)
            upd[place, :] = jnp.dot(scaled, b_act[...], preferred_element_type=jnp.float32)

    def advance(step, carry):
        @pl.when(step < CHUNKS)
        def _():
            updates(step)

        @pl.when(step >= CHUNKS)
        def _():
            within(order(step - CHUNKS))

        turn = lag + jnp.minimum(2 * (n // 2 - 1 - me) + 1, CHUNKS - 1)

        @pl.when(far_first & (step == turn))
        def _():
            pass_above()

        @pl.when(early & (step >= lag))
        def _():
            chain(step - lag)

        return carry

    @pl.when(me > 1)
    def _():
        set_up()

    loading(6).wait()
    lax.fori_loop(0, CHUNKS + lag, advance, 0)

    @pl.when(me <= 1)
    def _():
        set_up()

    ahead = jnp.where(early, lag, jnp.minimum(2 * (me - n // 2) + 2, CHUNKS))
    ahead = jnp.where(me == 0, CHUNKS // 2, ahead)

    def within_ahead(k, carry):
        within(k)
        return carry

    lax.fori_loop(lag, ahead, within_ahead, 0)

    @pl.when(me == 0)
    def _():
        pass_above()

    def outputs(step, carry):
        k = order(step)

        @pl.when(step >= ahead)
        def _():
            within(k)

        @pl.when(jnp.logical_not(early))
        def _():
            chain(k)

        squares = ssq[0:1, :]
        for j in range(blocks):
            place = block_place(k, j)
            outer = lax.dot_general(
                state_in[k, j * LANES : (j + 1) * LANES, :],
                c_act[...],
                (((1,), (1,)), ((), ())),
                preferred_element_type=jnp.float32,
            )
            gated = (pre[place, :] + block_rows(grow_rows, k, j) * outer) * z_t[place, :]
            squares = squares + jnp.sum(gated * gated, axis=0, keepdims=True)
            stage[k, j * LANES : (j + 1) * LANES, :] = gated.astype(jnp.bfloat16)
        ssq[0:1, :] = squares

        for part in range(parts):
            dest = k * parts + part

            @pl.when(dest != me)
            def _():
                out_copy(k, part, dest, me).start()

            @pl.when(dest == me)
            def _():
                own_out(k, part).start()

        return carry

    lax.fori_loop(0, CHUNKS, outputs, 0)

    scale = jnp.broadcast_to(lax.rsqrt(ssq[0:1, :] / width + EPS), (8, LANES))
    scale_out[...] = scale
    own_scale().start()

    def tell(other, carry):
        @pl.when(other != me)
        def _():
            scale_copy(other, me).start()

        return carry

    lax.fori_loop(0, n, tell, 0)

    def finish(source, carry):
        @pl.when(source != me)
        def _():
            out_copy(0, 0, source, source).wait_recv()
            scale_copy(source, source).wait_recv()

        @pl.when(source == me)
        def _():
            own_out(0, 0).wait()
            own_scale().wait()

        return carry

    lax.fori_loop(0, n, finish, 0)

    @pl.when(me < n - 1)
    def _():
        for index in range(2):
            halo_copy(index).wait_send()

        def drain_state(k, carry):
            halo_x_copy(k).wait_send()
            for p in range(pieces):
                state_copy(k, p).wait_send()
            return carry

        lax.fori_loop(0, CHUNKS, drain_state, 0)

    def drain(other, carry):
        @pl.when(other != me)
        def _():
            out_copy(0, 0, other, me).wait_send()
            scale_copy(other, me).wait_send()

        return carry

    lax.fori_loop(0, n, drain, 0)


def normalise(rows, gated_ref, scale_ref, gain_ref, out_ref, gain_col):
    me = lax.axis_index("ctx")
    step = pl.program_id(0)
    share = out_ref.shape[0]

    @pl.when(step == 0)
    def _():
        if rows % LANES == 0:
            own = gain_ref[:, pl.ds(pl.multiple_of(me * rows, LANES), rows)]
        else:
            own = gain_ref[pl.ds(me, 1), :]
        gain_col[...] = jnp.broadcast_to(own, (LANES, rows)).T

    gain = gain_col[pl.ds(pl.multiple_of(step * share, share), share), :]
    for i in range(gated_ref.shape[0]):
        value = gated_ref[i].astype(jnp.float32) * scale_ref[i, 0:1, :] * gain
        out_ref[:, i * SPAN : (i + 1) * SPAN] = value.astype(jnp.bfloat16)


def shards(
    x_in, z_in, b_in, c_in, dt_raw, dt_bias, a_log, d_skip, conv_x, conv_b, conv_c, norm_gain
):
    n = lax.axis_size("ctx")
    width = x_in.shape[1]
    state = b_in.shape[1]
    rows = width // n
    chunk = width // CHUNKS
    gain = norm_gain.reshape((1, width) if rows % LANES == 0 else (n, rows))
    taps = conv_x.shape[0]
    hbm = pl.BlockSpec(memory_space=pl.ANY)
    vmem = pl.BlockSpec(memory_space=pltpu.VMEM)
    f32, bf16 = jnp.float32, jnp.bfloat16
    dma = pltpu.SemaphoreType.DMA
    square = pltpu.VMEM((LANES, LANES), f32)
    gated, scales = pl.pallas_call(
        functools.partial(kernel, n),
        out_shape=(
            jax.ShapeDtypeStruct((n, rows, SPAN), bf16),
            jax.ShapeDtypeStruct((n, 8, LANES), f32),
        ),
        in_specs=[hbm] * 4 + [vmem] * 4 + [hbm] * 3,
        out_specs=(hbm, hbm),
        scratch_shapes=[
            pltpu.VMEM((SPAN, width), bf16),
            pltpu.VMEM((SPAN, width), bf16),
            pltpu.VMEM((SPAN, state), bf16),
            pltpu.VMEM((SPAN, state), bf16),
            pltpu.VMEM((taps, width), f32),
            pltpu.VMEM((taps, state), f32),
            pltpu.VMEM((taps, state), f32),
            pltpu.VMEM((HALO, width), bf16),
            pltpu.VMEM((HALO, state), bf16),
            pltpu.VMEM((HALO, state), bf16),
            pltpu.VMEM((SPAN + 24, LANES), f32),
            pltpu.VMEM((max(2, chunk // LANES), SPAN + 8, LANES), f32),
            pltpu.VMEM((width, SPAN), bf16),
            pltpu.VMEM((width, SPAN), f32),
            pltpu.VMEM((width, SPAN), f32),
            pltpu.VMEM((width, state), f32),
            pltpu.VMEM((CHUNKS, chunk, state), bf16),
            pltpu.VMEM((CHUNKS, chunk, state), bf16),
            pltpu.VMEM((CHUNKS, chunk, SPAN), bf16),
            pltpu.VMEM((8, LANES), f32),
            square,
            square,
            square,
            square,
            square,
            pltpu.VMEM((CHUNKS, SPAN, LANES), f32),
            square,
            square,
            pltpu.VMEM((SPAN, state), bf16),
            pltpu.VMEM((SPAN, state), bf16),
            pltpu.VMEM((8, LANES), f32),
            pltpu.SemaphoreType.REGULAR,
            dma((7,)),
            dma((CHUNKS + 2,)),
            dma((CHUNKS + 2,)),
            dma((CHUNKS, 2)),
            dma((CHUNKS, 2)),
            dma((n,)),
            dma((n,)),
            dma((n,)),
            dma((n,)),
        ],
        compiler_params=pltpu.CompilerParams(
            collective_id=0, has_side_effects=True, vmem_limit_bytes=56 * 1024 * 1024
        ),
        cost_estimate=pl.CostEstimate(
            flops=8 * SPAN * SPAN * width, bytes_accessed=6 * SPAN * width, transcendentals=0
        ),
    )(
        x_in,
        z_in,
        b_in,
        c_in,
        dt_raw.T,
        dt_bias[None, :],
        a_log[None, :],
        d_skip[None, :],
        conv_x,
        conv_b,
        conv_c,
    )
    share = rows // 2 if rows % 256 == 0 else rows
    return pl.pallas_call(
        functools.partial(normalise, rows),
        grid=(rows // share,),
        out_shape=jax.ShapeDtypeStruct((rows, n * SPAN), bf16),
        in_specs=[
            pl.BlockSpec((n, share, SPAN), lambda i: (0, i, 0)),
            pl.BlockSpec((n, 8, LANES), lambda i: (0, 0, 0)),
            pl.BlockSpec(gain.shape, lambda i: (0, 0)),
        ],
        out_specs=pl.BlockSpec((share, n * SPAN), lambda i: (i, 0)),
        scratch_shapes=[pltpu.VMEM((rows, LANES), f32)],
        compiler_params=pltpu.CompilerParams(vmem_limit_bytes=56 * 1024 * 1024),
    )(gated, scales, gain)


def solution(mesh):
    return jax.shard_map(
        shards,
        mesh=mesh,
        in_specs=(
            P("ctx", "tp"),
            P("ctx", "tp"),
            P("ctx", "tp"),
            P("ctx", "tp"),
            P("ctx", "tp"),
            P("tp"),
            P("tp"),
            P("tp"),
            P(None, "tp"),
            P(None, "tp"),
            P(None, "tp"),
            P("tp"),
        ),
        out_specs=P(("tp", "ctx"), None),
        check_vma=False,
    )
```

```python
import functools

import jax
import jax.numpy as jnp
from jax import lax
from jax.experimental import pallas as pl
from jax.experimental.pallas import tpu as pltpu
from jax.sharding import PartitionSpec as P

SPAN = 128
LANES = 128
HALO = 16
CHUNKS = 8
EPS = 1e-05
LOG2E = 1.4426950408889634
MESH = pl.DeviceIdType.MESH


def silu(value):
    half = 0.5 * value
    return half + half * jnp.tanh(half)


def conv_silu(pad, taps, count):
    total = taps[0:1] * pad[8 - count + 1 : 8 - count + 1 + SPAN, :]
    for tap in range(1, count):
        start = 8 - count + 1 + tap
        total = total + taps[tap : tap + 1] * pad[start : start + SPAN, :]
    return silu(total).astype(jnp.bfloat16)


def kernel(
    n,
    x_ref,
    z_ref,
    b_ref,
    c_ref,
    dt_ref,
    bias_ref,
    alog_ref,
    skip_ref,
    cx_ref,
    cb_ref,
    cc_ref,
    recv,
    scale_in,
    x_buf,
    z_buf,
    b_buf,
    c_buf,
    cx_buf,
    cb_buf,
    cc_buf,
    halo_x,
    halo_b,
    halo_c,
    small,
    pad,
    x_t,
    z_t,
    pre,
    upd,
    state_in,
    state_out,
    stage,
    scale_out,
    log_rows,
    mix_rows,
    grow_rows,
    last_rows,
    skip_rows,
    cols,
    turned_cols,
    scores,
    b_act,
    c_act,
    ssq,
    above,
    load,
    halo_send,
    halo_recv,
    state_send,
    state_recv,
    out_send,
    out_recv,
    scale_send,
    scale_recv,
):
    width = x_ref.shape[1]
    heads = dt_ref.shape[0]
    head = width // heads
    per_block = LANES // head
    chunk = width // CHUNKS
    blocks = chunk // LANES
    chunk_heads = heads // CHUNKS
    rows = width // n
    parts = chunk // rows
    taps = cx_ref.shape[0]
    me = lax.axis_index("ctx")
    nxt = lax.rem(me + 1, n)

    barrier = pltpu.get_barrier_semaphore()

    def greet(other):
        pl.semaphore_signal(barrier, inc=1, device_id={"ctx": other}, device_id_type=MESH)

    @pl.when(me > 0)
    def _():
        greet(me - 1)

    @pl.when(me < n - 1)
    def _():
        greet(me + 1)

    def tell_above():
        pl.semaphore_signal(above, inc=1, device_id={"ctx": me - 1}, device_id_type=MESH)

    def pass_above():
        pl.semaphore_wait(above, 1)

        @pl.when(me > 0)
        def _():
            tell_above()

    def halo_copy(index):
        source = (b_ref, c_ref)[index]
        target = (halo_b, halo_c)[index]
        return pltpu.make_async_remote_copy(
            src_ref=source.at[pl.ds(SPAN - HALO, HALO), :],
            dst_ref=target,
            send_sem=halo_send.at[CHUNKS + index],
            recv_sem=halo_recv.at[CHUNKS + index],
            device_id={"ctx": nxt},
            device_id_type=MESH,
        )

    def halo_x_copy(k):
        place = pl.ds(pl.multiple_of(k * chunk, LANES), chunk)
        return pltpu.make_async_remote_copy(
            src_ref=x_ref.at[pl.ds(SPAN - HALO, HALO), place],
            dst_ref=halo_x.at[:, place],
            send_sem=halo_send.at[k],
            recv_sem=halo_recv.at[k],
            device_id={"ctx": nxt},
            device_id_type=MESH,
        )

    pieces = min(2, blocks)
    piece = chunk // pieces

    def state_copy(k, p):
        return pltpu.make_async_remote_copy(
            src_ref=state_out.at[k, pl.ds(p * piece, piece), :],
            dst_ref=state_in.at[k, pl.ds(p * piece, piece), :],
            send_sem=state_send.at[k, p],
            recv_sem=state_recv.at[k, p],
            device_id={"ctx": nxt},
            device_id_type=MESH,
        )

    def out_copy(k, part, dest, slot):
        return pltpu.make_async_remote_copy(
            src_ref=stage.at[k, pl.ds(part * rows, rows), :],
            dst_ref=recv.at[slot],
            send_sem=out_send.at[dest],
            recv_sem=out_recv.at[slot],
            device_id={"ctx": dest},
            device_id_type=MESH,
        )

    def own_out(k, part):
        return pltpu.make_async_copy(
            stage.at[k, pl.ds(part * rows, rows), :], recv.at[me], out_recv.at[me]
        )

    def own_scale():
        return pltpu.make_async_copy(scale_out, scale_in.at[me], scale_recv.at[me])

    def scale_copy(dest, slot):
        return pltpu.make_async_remote_copy(
            src_ref=scale_out,
            dst_ref=scale_in.at[slot],
            send_sem=scale_send.at[dest],
            recv_sem=scale_recv.at[slot],
            device_id={"ctx": dest},
            device_id_type=MESH,
        )

    def loading(index):
        source = (x_ref, b_ref, c_ref, cx_ref, cb_ref, cc_ref, z_ref)[index]
        target = (x_buf, b_buf, c_buf, cx_buf, cb_buf, cc_buf, z_buf)[index]
        return pltpu.make_async_copy(source, target, load.at[index])

    for index in range(7):
        loading(index).start()

    def down_columns(row, count):
        return jnp.broadcast_to(row, (SPAN, count)).T

    small[...] = jnp.zeros_like(small)
    small[SPAN : SPAN + 1, 0:heads] = bias_ref[...]
    small[SPAN + 8 : SPAN + 9, 0:heads] = alog_ref[...]
    small[SPAN + 16 : SPAN + 17, 0:heads] = skip_ref[...]
    small[0:heads, :] = dt_ref[...]
    raw = small[0:SPAN, :] + down_columns(small[SPAN : SPAN + 1, :], LANES)
    delta = jnp.maximum(raw, 0.0) + jnp.log1p(jnp.exp(-jnp.abs(raw)))
    rate = -down_columns(jnp.exp(small[SPAN + 8 : SPAN + 9, :]), LANES) * delta
    down = lax.broadcasted_iota(jnp.int32, (SPAN, SPAN), 0)
    across = lax.broadcasted_iota(jnp.int32, (SPAN, SPAN), 1)
    upper = jnp.where(down <= across, 1.0, 0.0)
    logs = jnp.dot(
        rate, upper, precision=lax.Precision.HIGHEST, preferred_element_type=jnp.float32
    )
    last = jnp.broadcast_to(logs[:, SPAN - 1 : SPAN], (SPAN, LANES))
    log_rows[...] = logs * LOG2E
    mix_rows[...] = jnp.exp(last - logs) * delta
    last_rows[...] = jnp.exp(last)
    turned_cols[...] = (logs - jnp.log(delta)) * LOG2E

    ends = (me == 0) | (me == n - 1)

    @pl.when(ends)
    def _():
        pl.semaphore_wait(barrier, 1)

    @pl.when(jnp.logical_not(ends))
    def _():
        pl.semaphore_wait(barrier, 2)

    @pl.when(me == n - 1)
    def _():
        tell_above()

    @pl.when(me < n - 1)
    def _():
        halo_copy(0).start()
        halo_x_copy(0).start()
        halo_copy(1).start()
        for k in range(1, CHUNKS):
            halo_x_copy(k).start()

    early = me < n // 2

    @pl.when(jnp.logical_not(early) & (me < n - 1))
    def _():
        pass_above()

    for index in range(6):
        loading(index).wait()

    @pl.when(me > 0)
    def _():
        halo_copy(0).wait_recv()

    @pl.when(me == 0)
    def _():
        halo_x[...] = jnp.zeros_like(halo_x)
        halo_b[...] = jnp.zeros_like(halo_b)
        halo_c[...] = jnp.zeros_like(halo_c)
        state_in[...] = jnp.zeros_like(state_in)

    def project(slot, source, halo, weights, target):
        pad[slot, 0:8, :] = halo[...].astype(jnp.float32)[HALO - 8 :]
        pad[slot, 8 : 8 + SPAN, :] = source[...].astype(jnp.float32)
        target[...] = conv_silu(pad.at[slot], weights[...], taps)

    project(0, b_buf, halo_b, cb_buf, b_act)

    def head_row(ref, index):
        return jnp.broadcast_to(ref[pl.ds(index, 1), :], (head, LANES))

    def block_rows(ref, k, j):
        first = k * chunk_heads + j * per_block
        return jnp.concatenate([head_row(ref, first + i) for i in range(per_block)], axis=0)

    def block_place(k, j):
        return pl.ds(pl.multiple_of(k * chunk + j * LANES, LANES), LANES)

    def chain(k):
        for p in range(pieces):

            @pl.when(me > 0)
            def _():
                state_copy(k, p).wait_recv()

            @pl.when(me < n - 1)
            def _():
                for j in range(p * piece // LANES, (p + 1) * piece // LANES):
                    entering = state_in[k, j * LANES : (j + 1) * LANES, :].astype(jnp.float32)
                    leaving = block_rows(last_rows, k, j) * entering + upd[block_place(k, j), :]
                    state_out[k, j * LANES : (j + 1) * LANES, :] = leaving.astype(jnp.bfloat16)
                state_copy(k, p).start()

    def set_up():
        @pl.when(me > 0)
        def _():
            halo_copy(1).wait_recv()

        project(1, c_buf, halo_c, cc_buf, c_act)
        overlap = lax.dot_general(
            b_act[...], c_act[...], (((1,), (1,)), ((), ())), preferred_element_type=jnp.float32
        )
        scores[...] = jnp.where(down <= across, overlap, 0.0)
        grow_rows[...] = jnp.exp2(log_rows[...])
        skip_rows[...] = down_columns(small[SPAN + 16 : SPAN + 17, :], LANES)
        shifted = turned_cols[...].T
        for k in range(CHUNKS):
            cols[k, :, 0:chunk_heads] = shifted[:, k * chunk_heads : (k + 1) * chunk_heads]
        ssq[...] = jnp.zeros_like(ssq)

    def within(k):
        shifts = cols[k]
        for j in range(blocks):
            place = block_place(k, j)
            z_t[place, :] = silu(z_buf[:, place].T.astype(jnp.float32))
            x_block = x_t[place, :]
            inner = []
            for i in range(per_block):
                which = j * per_block + i
                gap = (
                    log_rows[pl.ds(k * chunk_heads + which, 1), :] - shifts[:, which : which + 1]
                )
                weights = (scores[...] * jnp.exp2(gap)).astype(jnp.bfloat16)
                inner.append(
                    jnp.dot(
                        x_block[i * head : (i + 1) * head],
                        weights,
                        preferred_element_type=jnp.float32,
                    )
                )
            pre[place, :] = jnp.concatenate(inner, axis=0) + block_rows(
                skip_rows, k, j
            ) * x_block.astype(jnp.float32)

    middle = early & (me > 0)
    lag = jnp.where(middle, jnp.minimum(2 * (me - 1), CHUNKS), 0)

    def updates(k):
        @pl.when(me > 0)
        def _():
            halo_x_copy(k).wait_recv()

        for j in range(blocks):
            place = block_place(k, j)
            pad[j, 0:8, :] = halo_x[:, place].astype(jnp.float32)[HALO - 8 :]
            pad[j, 8 : 8 + SPAN, :] = x_buf[:, place].astype(jnp.float32)
            act = conv_silu(pad.at[j], cx_buf[:, place], taps)
            turned = act.T
            x_t[place, :] = turned
            scaled = (turned.astype(jnp.float32) * block_rows(mix_rows, k, j)).astype(jnp.bfloat16)
            upd[place, :] = jnp.dot(scaled, b_act[...], preferred_element_type=jnp.float32)

    def advance(step, carry):
        @pl.when(step < CHUNKS)
        def _():
            updates(step)

        @pl.when(step >= CHUNKS)
        def _():
            within(step - CHUNKS)

        turn = lag + jnp.minimum(2 * (n // 2 - 1 - me) + 1, CHUNKS - 1)

        @pl.when(middle & (step == turn))
        def _():
            pass_above()

        @pl.when(early & (step >= lag))
        def _():
            chain(step - lag)

        return carry

    @pl.when(me > 1)
    def _():
        set_up()

    loading(6).wait()
    lax.fori_loop(0, CHUNKS + lag, advance, 0)

    @pl.when(me <= 1)
    def _():
        set_up()

    ahead = jnp.where(early, lag, jnp.minimum(2 * (me - n // 2) + 2, CHUNKS))
    ahead = jnp.where(me == 0, CHUNKS // 2, ahead)

    def within_ahead(k, carry):
        within(k)
        return carry

    lax.fori_loop(lag, ahead, within_ahead, 0)

    @pl.when(me == 0)
    def _():
        pass_above()

    def outputs(k, carry):
        @pl.when(k >= ahead)
        def _():
            within(k)

        @pl.when(jnp.logical_not(early))
        def _():
            chain(k)

        squares = ssq[0:1, :]
        for j in range(blocks):
            place = block_place(k, j)
            outer = lax.dot_general(
                state_in[k, j * LANES : (j + 1) * LANES, :],
                c_act[...],
                (((1,), (1,)), ((), ())),
                preferred_element_type=jnp.float32,
            )
            gated = (pre[place, :] + block_rows(grow_rows, k, j) * outer) * z_t[place, :]
            squares = squares + jnp.sum(gated * gated, axis=0, keepdims=True)
            stage[k, j * LANES : (j + 1) * LANES, :] = gated.astype(jnp.bfloat16)
        ssq[0:1, :] = squares

        for part in range(parts):
            dest = k * parts + part

            @pl.when(dest != me)
            def _():
                out_copy(k, part, dest, me).start()

            @pl.when(dest == me)
            def _():
                own_out(k, part).start()

        return carry

    lax.fori_loop(0, CHUNKS, outputs, 0)

    scale = jnp.broadcast_to(lax.rsqrt(ssq[0:1, :] / width + EPS), (8, LANES))
    scale_out[...] = scale
    own_scale().start()

    def tell(other, carry):
        @pl.when(other != me)
        def _():
            scale_copy(other, me).start()

        return carry

    lax.fori_loop(0, n, tell, 0)

    def finish(source, carry):
        @pl.when(source != me)
        def _():
            out_copy(0, 0, source, source).wait_recv()
            scale_copy(source, source).wait_recv()

        @pl.when(source == me)
        def _():
            own_out(0, 0).wait()
            own_scale().wait()

        return carry

    lax.fori_loop(0, n, finish, 0)

    @pl.when(me < n - 1)
    def _():
        for index in range(2):
            halo_copy(index).wait_send()

        def drain_state(k, carry):
            halo_x_copy(k).wait_send()
            for p in range(pieces):
                state_copy(k, p).wait_send()
            return carry

        lax.fori_loop(0, CHUNKS, drain_state, 0)

    def drain(other, carry):
        @pl.when(other != me)
        def _():
            out_copy(0, 0, other, me).wait_send()
            scale_copy(other, me).wait_send()

        return carry

    lax.fori_loop(0, n, drain, 0)


def normalise(rows, gated_ref, scale_ref, gain_ref, out_ref, gain_col):
    me = lax.axis_index("ctx")
    step = pl.program_id(0)
    share = out_ref.shape[0]

    @pl.when(step == 0)
    def _():
        if rows % LANES == 0:
            own = gain_ref[:, pl.ds(pl.multiple_of(me * rows, LANES), rows)]
        else:
            own = gain_ref[pl.ds(me, 1), :]
        gain_col[...] = jnp.broadcast_to(own, (LANES, rows)).T

    gain = gain_col[pl.ds(pl.multiple_of(step * share, share), share), :]
    for i in range(gated_ref.shape[0]):
        value = gated_ref[i].astype(jnp.float32) * scale_ref[i, 0:1, :] * gain
        out_ref[:, i * SPAN : (i + 1) * SPAN] = value.astype(jnp.bfloat16)


def shards(
    x_in, z_in, b_in, c_in, dt_raw, dt_bias, a_log, d_skip, conv_x, conv_b, conv_c, norm_gain
):
    n = lax.axis_size("ctx")
    width = x_in.shape[1]
    state = b_in.shape[1]
    rows = width // n
    chunk = width // CHUNKS
    gain = norm_gain.reshape((1, width) if rows % LANES == 0 else (n, rows))
    taps = conv_x.shape[0]
    hbm = pl.BlockSpec(memory_space=pl.ANY)
    vmem = pl.BlockSpec(memory_space=pltpu.VMEM)
    f32, bf16 = jnp.float32, jnp.bfloat16
    dma = pltpu.SemaphoreType.DMA
    square = pltpu.VMEM((LANES, LANES), f32)
    gated, scales = pl.pallas_call(
        functools.partial(kernel, n),
        out_shape=(
            jax.ShapeDtypeStruct((n, rows, SPAN), bf16),
            jax.ShapeDtypeStruct((n, 8, LANES), f32),
        ),
        in_specs=[hbm] * 4 + [vmem] * 4 + [hbm] * 3,
        out_specs=(hbm, hbm),
        scratch_shapes=[
            pltpu.VMEM((SPAN, width), bf16),
            pltpu.VMEM((SPAN, width), bf16),
            pltpu.VMEM((SPAN, state), bf16),
            pltpu.VMEM((SPAN, state), bf16),
            pltpu.VMEM((taps, width), f32),
            pltpu.VMEM((taps, state), f32),
            pltpu.VMEM((taps, state), f32),
            pltpu.VMEM((HALO, width), bf16),
            pltpu.VMEM((HALO, state), bf16),
            pltpu.VMEM((HALO, state), bf16),
            pltpu.VMEM((SPAN + 24, LANES), f32),
            pltpu.VMEM((max(2, chunk // LANES), SPAN + 8, LANES), f32),
            pltpu.VMEM((width, SPAN), bf16),
            pltpu.VMEM((width, SPAN), f32),
            pltpu.VMEM((width, SPAN), f32),
            pltpu.VMEM((width, state), f32),
            pltpu.VMEM((CHUNKS, chunk, state), bf16),
            pltpu.VMEM((CHUNKS, chunk, state), bf16),
            pltpu.VMEM((CHUNKS, chunk, SPAN), bf16),
            pltpu.VMEM((8, LANES), f32),
            square,
            square,
            square,
            square,
            square,
            pltpu.VMEM((CHUNKS, SPAN, LANES), f32),
            square,
            square,
            pltpu.VMEM((SPAN, state), bf16),
            pltpu.VMEM((SPAN, state), bf16),
            pltpu.VMEM((8, LANES), f32),
            pltpu.SemaphoreType.REGULAR,
            dma((7,)),
            dma((CHUNKS + 2,)),
            dma((CHUNKS + 2,)),
            dma((CHUNKS, 2)),
            dma((CHUNKS, 2)),
            dma((n,)),
            dma((n,)),
            dma((n,)),
            dma((n,)),
        ],
        compiler_params=pltpu.CompilerParams(
            collective_id=0, has_side_effects=True, vmem_limit_bytes=56 * 1024 * 1024
        ),
        cost_estimate=pl.CostEstimate(
            flops=8 * SPAN * SPAN * width, bytes_accessed=6 * SPAN * width, transcendentals=0
        ),
    )(
        x_in,
        z_in,
        b_in,
        c_in,
        dt_raw.T,
        dt_bias[None, :],
        a_log[None, :],
        d_skip[None, :],
        conv_x,
        conv_b,
        conv_c,
    )
    share = rows // 2 if rows % 256 == 0 else rows
    return pl.pallas_call(
        functools.partial(normalise, rows),
        grid=(rows // share,),
        out_shape=jax.ShapeDtypeStruct((rows, n * SPAN), bf16),
        in_specs=[
            pl.BlockSpec((n, share, SPAN), lambda i: (0, i, 0)),
            pl.BlockSpec((n, 8, LANES), lambda i: (0, 0, 0)),
            pl.BlockSpec(gain.shape, lambda i: (0, 0)),
        ],
        out_specs=pl.BlockSpec((share, n * SPAN), lambda i: (i, 0)),
        scratch_shapes=[pltpu.VMEM((rows, LANES), f32)],
        compiler_params=pltpu.CompilerParams(vmem_limit_bytes=56 * 1024 * 1024),
    )(gated, scales, gain)


def solution(mesh):
    return jax.shard_map(
        shards,
        mesh=mesh,
        in_specs=(
            P("ctx", "tp"),
            P("ctx", "tp"),
            P("ctx", "tp"),
            P("ctx", "tp"),
            P("ctx", "tp"),
            P("tp"),
            P("tp"),
            P("tp"),
            P(None, "tp"),
            P(None, "tp"),
            P(None, "tp"),
            P("tp"),
        ),
        out_specs=P(("tp", "ctx"), None),
        check_vma=False,
    )
```

```python
import functools

import jax
import jax.numpy as jnp
from jax import lax
from jax.experimental import pallas as pl
from jax.experimental.pallas import tpu as pltpu
from jax.sharding import PartitionSpec as P

SPAN = 128
LANES = 128
HALO = 16
CHUNKS = 8
EPS = 1e-05
LOG2E = 1.4426950408889634
MESH = pl.DeviceIdType.MESH


def silu(value):
    half = 0.5 * value
    return half + half * jnp.tanh(half)


def conv_silu(pad, taps, count):
    total = taps[0:1] * pad[8 - count + 1 : 8 - count + 1 + SPAN, :]
    for tap in range(1, count):
        start = 8 - count + 1 + tap
        total = total + taps[tap : tap + 1] * pad[start : start + SPAN, :]
    return silu(total).astype(jnp.bfloat16)


def kernel(
    n,
    x_ref,
    z_ref,
    b_ref,
    c_ref,
    dt_ref,
    bias_ref,
    alog_ref,
    skip_ref,
    cx_ref,
    cb_ref,
    cc_ref,
    recv,
    scale_in,
    x_buf,
    z_buf,
    b_buf,
    c_buf,
    cx_buf,
    cb_buf,
    cc_buf,
    halo_x,
    halo_b,
    halo_c,
    small,
    pad,
    x_t,
    z_t,
    pre,
    upd,
    state_in,
    state_out,
    stage,
    scale_out,
    log_rows,
    mix_rows,
    grow_rows,
    last_rows,
    skip_rows,
    cols,
    turned_cols,
    scores,
    b_act,
    c_act,
    ssq,
    above,
    load,
    halo_send,
    halo_recv,
    state_send,
    state_recv,
    out_send,
    out_recv,
    scale_send,
    scale_recv,
):
    width = x_ref.shape[1]
    heads = dt_ref.shape[0]
    head = width // heads
    per_block = LANES // head
    chunk = width // CHUNKS
    blocks = chunk // LANES
    chunk_heads = heads // CHUNKS
    rows = width // n
    parts = chunk // rows
    taps = cx_ref.shape[0]
    me = lax.axis_index("ctx")
    nxt = lax.rem(me + 1, n)

    barrier = pltpu.get_barrier_semaphore()

    def greet(other):
        pl.semaphore_signal(barrier, inc=1, device_id={"ctx": other}, device_id_type=MESH)

    @pl.when(me > 0)
    def _():
        greet(me - 1)

    @pl.when(me < n - 1)
    def _():
        greet(me + 1)

    def tell_above():
        pl.semaphore_signal(above, inc=1, device_id={"ctx": me - 1}, device_id_type=MESH)

    def pass_above():
        pl.semaphore_wait(above, 1)

        @pl.when(me > 0)
        def _():
            tell_above()

    def halo_copy(index):
        source = (b_ref, c_ref)[index]
        target = (halo_b, halo_c)[index]
        return pltpu.make_async_remote_copy(
            src_ref=source.at[pl.ds(SPAN - HALO, HALO), :],
            dst_ref=target,
            send_sem=halo_send.at[CHUNKS + index],
            recv_sem=halo_recv.at[CHUNKS + index],
            device_id={"ctx": nxt},
            device_id_type=MESH,
        )

    def halo_x_copy(k):
        place = pl.ds(pl.multiple_of(k * chunk, LANES), chunk)
        return pltpu.make_async_remote_copy(
            src_ref=x_ref.at[pl.ds(SPAN - HALO, HALO), place],
            dst_ref=halo_x.at[:, place],
            send_sem=halo_send.at[k],
            recv_sem=halo_recv.at[k],
            device_id={"ctx": nxt},
            device_id_type=MESH,
        )

    pieces = min(2, blocks)
    piece = chunk // pieces

    def state_copy(k, p):
        return pltpu.make_async_remote_copy(
            src_ref=state_out.at[k, pl.ds(p * piece, piece), :],
            dst_ref=state_in.at[k, pl.ds(p * piece, piece), :],
            send_sem=state_send.at[k, p],
            recv_sem=state_recv.at[k, p],
            device_id={"ctx": nxt},
            device_id_type=MESH,
        )

    def out_copy(k, part, dest, slot):
        return pltpu.make_async_remote_copy(
            src_ref=stage.at[k, pl.ds(part * rows, rows), :],
            dst_ref=recv.at[slot],
            send_sem=out_send.at[dest],
            recv_sem=out_recv.at[slot],
            device_id={"ctx": dest},
            device_id_type=MESH,
        )

    def own_out(k, part):
        return pltpu.make_async_copy(
            stage.at[k, pl.ds(part * rows, rows), :], recv.at[me], out_recv.at[me]
        )

    def own_scale():
        return pltpu.make_async_copy(scale_out, scale_in.at[me], scale_recv.at[me])

    def scale_copy(dest, slot):
        return pltpu.make_async_remote_copy(
            src_ref=scale_out,
            dst_ref=scale_in.at[slot],
            send_sem=scale_send.at[dest],
            recv_sem=scale_recv.at[slot],
            device_id={"ctx": dest},
            device_id_type=MESH,
        )

    def loading(index):
        source = (x_ref, b_ref, c_ref, cx_ref, cb_ref, cc_ref, z_ref)[index]
        target = (x_buf, b_buf, c_buf, cx_buf, cb_buf, cc_buf, z_buf)[index]
        return pltpu.make_async_copy(source, target, load.at[index])

    for index in range(7):
        loading(index).start()

    def down_columns(row, count):
        return jnp.broadcast_to(row, (SPAN, count)).T

    small[...] = jnp.zeros_like(small)
    small[SPAN : SPAN + 1, 0:heads] = bias_ref[...]
    small[SPAN + 8 : SPAN + 9, 0:heads] = alog_ref[...]
    small[SPAN + 16 : SPAN + 17, 0:heads] = skip_ref[...]
    small[0:heads, :] = dt_ref[...]
    raw = small[0:SPAN, :] + down_columns(small[SPAN : SPAN + 1, :], LANES)
    delta = jnp.maximum(raw, 0.0) + jnp.log1p(jnp.exp(-jnp.abs(raw)))
    rate = -down_columns(jnp.exp(small[SPAN + 8 : SPAN + 9, :]), LANES) * delta
    down = lax.broadcasted_iota(jnp.int32, (SPAN, SPAN), 0)
    across = lax.broadcasted_iota(jnp.int32, (SPAN, SPAN), 1)
    upper = jnp.where(down <= across, 1.0, 0.0)
    logs = jnp.dot(
        rate, upper, precision=lax.Precision.HIGHEST, preferred_element_type=jnp.float32
    )
    last = jnp.broadcast_to(logs[:, SPAN - 1 : SPAN], (SPAN, LANES))
    log_rows[...] = logs * LOG2E
    mix_rows[...] = jnp.exp(last - logs) * delta
    last_rows[...] = jnp.exp(last)
    turned_cols[...] = (logs - jnp.log(delta)) * LOG2E

    ends = (me == 0) | (me == n - 1)

    @pl.when(ends)
    def _():
        pl.semaphore_wait(barrier, 1)

    @pl.when(jnp.logical_not(ends))
    def _():
        pl.semaphore_wait(barrier, 2)

    @pl.when(me == n - 1)
    def _():
        tell_above()

    @pl.when(me < n - 1)
    def _():
        halo_copy(0).start()
        halo_x_copy(0).start()
        halo_copy(1).start()
        for k in range(1, CHUNKS):
            halo_x_copy(k).start()

    early = me < n // 2

    @pl.when(jnp.logical_not(early) & (me < n - 1))
    def _():
        pass_above()

    for index in range(6):
        loading(index).wait()

    @pl.when(me > 0)
    def _():
        halo_copy(0).wait_recv()

    @pl.when(me == 0)
    def _():
        halo_x[...] = jnp.zeros_like(halo_x)
        halo_b[...] = jnp.zeros_like(halo_b)
        halo_c[...] = jnp.zeros_like(halo_c)
        state_in[...] = jnp.zeros_like(state_in)

    def project(slot, source, halo, weights, target):
        pad[slot, 0:8, :] = halo[...].astype(jnp.float32)[HALO - 8 :]
        pad[slot, 8 : 8 + SPAN, :] = source[...].astype(jnp.float32)
        target[...] = conv_silu(pad.at[slot], weights[...], taps)

    project(0, b_buf, halo_b, cb_buf, b_act)

    def head_row(ref, index):
        return jnp.broadcast_to(ref[pl.ds(index, 1), :], (head, LANES))

    def block_rows(ref, k, j):
        first = k * chunk_heads + j * per_block
        return jnp.concatenate([head_row(ref, first + i) for i in range(per_block)], axis=0)

    def block_place(k, j):
        return pl.ds(pl.multiple_of(k * chunk + j * LANES, LANES), LANES)

    def chain(k):
        for p in range(pieces):

            @pl.when(me > 0)
            def _():
                state_copy(k, p).wait_recv()

            @pl.when(me < n - 1)
            def _():
                for j in range(p * piece // LANES, (p + 1) * piece // LANES):
                    entering = state_in[k, j * LANES : (j + 1) * LANES, :].astype(jnp.float32)
                    leaving = block_rows(last_rows, k, j) * entering + upd[block_place(k, j), :]
                    state_out[k, j * LANES : (j + 1) * LANES, :] = leaving.astype(jnp.bfloat16)
                state_copy(k, p).start()

    def set_up():
        @pl.when(me > 0)
        def _():
            halo_copy(1).wait_recv()

        project(1, c_buf, halo_c, cc_buf, c_act)
        overlap = lax.dot_general(
            b_act[...], c_act[...], (((1,), (1,)), ((), ())), preferred_element_type=jnp.float32
        )
        scores[...] = jnp.where(down <= across, overlap, 0.0)
        grow_rows[...] = jnp.exp2(log_rows[...])
        skip_rows[...] = down_columns(small[SPAN + 16 : SPAN + 17, :], LANES)
        shifted = turned_cols[...].T
        for k in range(CHUNKS):
            cols[k, :, 0:chunk_heads] = shifted[:, k * chunk_heads : (k + 1) * chunk_heads]
        ssq[...] = jnp.zeros_like(ssq)

    def within(k):
        shifts = cols[k]
        for j in range(blocks):
            place = block_place(k, j)
            z_t[place, :] = silu(z_buf[:, place].T.astype(jnp.float32))
            x_block = x_t[place, :]
            inner = []
            for i in range(per_block):
                which = j * per_block + i
                gap = (
                    log_rows[pl.ds(k * chunk_heads + which, 1), :] - shifts[:, which : which + 1]
                )
                weights = (scores[...] * jnp.exp2(gap)).astype(jnp.bfloat16)
                inner.append(
                    jnp.dot(
                        x_block[i * head : (i + 1) * head],
                        weights,
                        preferred_element_type=jnp.float32,
                    )
                )
            pre[place, :] = jnp.concatenate(inner, axis=0) + block_rows(
                skip_rows, k, j
            ) * x_block.astype(jnp.float32)

    middle = early & (me > 0)
    lag = jnp.where(middle, jnp.minimum(2 * (me - 1), CHUNKS), 0)

    far_first = me == n // 2 - 1

    def order(step):
        return jnp.where(far_first, lax.rem(step + CHUNKS // 2, CHUNKS), step)

    def updates(k):
        @pl.when(me > 0)
        def _():
            halo_x_copy(k).wait_recv()

        for j in range(blocks):
            place = block_place(k, j)
            pad[j, 0:8, :] = halo_x[:, place].astype(jnp.float32)[HALO - 8 :]
            pad[j, 8 : 8 + SPAN, :] = x_buf[:, place].astype(jnp.float32)
            act = conv_silu(pad.at[j], cx_buf[:, place], taps)
            turned = act.T
            x_t[place, :] = turned
            scaled = (turned.astype(jnp.float32) * block_rows(mix_rows, k, j)).astype(jnp.bfloat16)
            upd[place, :] = jnp.dot(scaled, b_act[...], preferred_element_type=jnp.float32)

    def advance(step, carry):
        @pl.when(step < CHUNKS)
        def _():
            updates(step)

        @pl.when(step >= CHUNKS)
        def _():
            within(order(step - CHUNKS))

        turn = lag + jnp.minimum(2 * (n // 2 - 1 - me) + 1, CHUNKS - 1)

        @pl.when(middle & (step == turn))
        def _():
            pass_above()

        @pl.when(early & (step >= lag))
        def _():
            chain(step - lag)

        return carry

    @pl.when(me > 1)
    def _():
        set_up()

    loading(6).wait()
    lax.fori_loop(0, CHUNKS + lag, advance, 0)

    @pl.when(me <= 1)
    def _():
        set_up()

    ahead = jnp.where(early, lag, jnp.minimum(2 * (me - n // 2) + 2, CHUNKS))
    ahead = jnp.where(me == 0, CHUNKS // 2, ahead)

    def within_ahead(k, carry):
        within(k)
        return carry

    lax.fori_loop(lag, ahead, within_ahead, 0)

    @pl.when(me == 0)
    def _():
        pass_above()

    def outputs(step, carry):
        k = order(step)

        @pl.when(step >= ahead)
        def _():
            within(k)

        @pl.when(jnp.logical_not(early))
        def _():
            chain(k)

        squares = ssq[0:1, :]
        for j in range(blocks):
            place = block_place(k, j)
            outer = lax.dot_general(
                state_in[k, j * LANES : (j + 1) * LANES, :],
                c_act[...],
                (((1,), (1,)), ((), ())),
                preferred_element_type=jnp.float32,
            )
            gated = (pre[place, :] + block_rows(grow_rows, k, j) * outer) * z_t[place, :]
            squares = squares + jnp.sum(gated * gated, axis=0, keepdims=True)
            stage[k, j * LANES : (j + 1) * LANES, :] = gated.astype(jnp.bfloat16)
        ssq[0:1, :] = squares

        for part in range(parts):
            dest = k * parts + part

            @pl.when(dest != me)
            def _():
                out_copy(k, part, dest, me).start()

            @pl.when(dest == me)
            def _():
                own_out(k, part).start()

        return carry

    lax.fori_loop(0, CHUNKS, outputs, 0)

    scale = jnp.broadcast_to(lax.rsqrt(ssq[0:1, :] / width + EPS), (8, LANES))
    scale_out[...] = scale
    own_scale().start()

    def tell(other, carry):
        @pl.when(other != me)
        def _():
            scale_copy(other, me).start()

        return carry

    lax.fori_loop(0, n, tell, 0)

    def finish(source, carry):
        @pl.when(source != me)
        def _():
            out_copy(0, 0, source, source).wait_recv()
            scale_copy(source, source).wait_recv()

        @pl.when(source == me)
        def _():
            own_out(0, 0).wait()
            own_scale().wait()

        return carry

    lax.fori_loop(0, n, finish, 0)

    @pl.when(me < n - 1)
    def _():
        for index in range(2):
            halo_copy(index).wait_send()

        def drain_state(k, carry):
            halo_x_copy(k).wait_send()
            for p in range(pieces):
                state_copy(k, p).wait_send()
            return carry

        lax.fori_loop(0, CHUNKS, drain_state, 0)

    def drain(other, carry):
        @pl.when(other != me)
        def _():
            out_copy(0, 0, other, me).wait_send()
            scale_copy(other, me).wait_send()

        return carry

    lax.fori_loop(0, n, drain, 0)


def normalise(rows, gated_ref, scale_ref, gain_ref, out_ref, gain_col):
    me = lax.axis_index("ctx")
    step = pl.program_id(0)
    share = out_ref.shape[0]

    @pl.when(step == 0)
    def _():
        if rows % LANES == 0:
            own = gain_ref[:, pl.ds(pl.multiple_of(me * rows, LANES), rows)]
        else:
            own = gain_ref[pl.ds(me, 1), :]
        gain_col[...] = jnp.broadcast_to(own, (LANES, rows)).T

    gain = gain_col[pl.ds(pl.multiple_of(step * share, share), share), :]
    for i in range(gated_ref.shape[0]):
        value = gated_ref[i].astype(jnp.float32) * scale_ref[i, 0:1, :] * gain
        out_ref[:, i * SPAN : (i + 1) * SPAN] = value.astype(jnp.bfloat16)


def shards(
    x_in, z_in, b_in, c_in, dt_raw, dt_bias, a_log, d_skip, conv_x, conv_b, conv_c, norm_gain
):
    n = lax.axis_size("ctx")
    width = x_in.shape[1]
    state = b_in.shape[1]
    rows = width // n
    chunk = width // CHUNKS
    gain = norm_gain.reshape((1, width) if rows % LANES == 0 else (n, rows))
    taps = conv_x.shape[0]
    hbm = pl.BlockSpec(memory_space=pl.ANY)
    vmem = pl.BlockSpec(memory_space=pltpu.VMEM)
    f32, bf16 = jnp.float32, jnp.bfloat16
    dma = pltpu.SemaphoreType.DMA
    square = pltpu.VMEM((LANES, LANES), f32)
    gated, scales = pl.pallas_call(
        functools.partial(kernel, n),
        out_shape=(
            jax.ShapeDtypeStruct((n, rows, SPAN), bf16),
            jax.ShapeDtypeStruct((n, 8, LANES), f32),
        ),
        in_specs=[hbm] * 4 + [vmem] * 4 + [hbm] * 3,
        out_specs=(hbm, hbm),
        scratch_shapes=[
            pltpu.VMEM((SPAN, width), bf16),
            pltpu.VMEM((SPAN, width), bf16),
            pltpu.VMEM((SPAN, state), bf16),
            pltpu.VMEM((SPAN, state), bf16),
            pltpu.VMEM((taps, width), f32),
            pltpu.VMEM((taps, state), f32),
            pltpu.VMEM((taps, state), f32),
            pltpu.VMEM((HALO, width), bf16),
            pltpu.VMEM((HALO, state), bf16),
            pltpu.VMEM((HALO, state), bf16),
            pltpu.VMEM((SPAN + 24, LANES), f32),
            pltpu.VMEM((max(2, chunk // LANES), SPAN + 8, LANES), f32),
            pltpu.VMEM((width, SPAN), bf16),
            pltpu.VMEM((width, SPAN), f32),
            pltpu.VMEM((width, SPAN), f32),
            pltpu.VMEM((width, state), f32),
            pltpu.VMEM((CHUNKS, chunk, state), bf16),
            pltpu.VMEM((CHUNKS, chunk, state), bf16),
            pltpu.VMEM((CHUNKS, chunk, SPAN), bf16),
            pltpu.VMEM((8, LANES), f32),
            square,
            square,
            square,
            square,
            square,
            pltpu.VMEM((CHUNKS, SPAN, LANES), f32),
            square,
            square,
            pltpu.VMEM((SPAN, state), bf16),
            pltpu.VMEM((SPAN, state), bf16),
            pltpu.VMEM((8, LANES), f32),
            pltpu.SemaphoreType.REGULAR,
            dma((7,)),
            dma((CHUNKS + 2,)),
            dma((CHUNKS + 2,)),
            dma((CHUNKS, 2)),
            dma((CHUNKS, 2)),
            dma((n,)),
            dma((n,)),
            dma((n,)),
            dma((n,)),
        ],
        compiler_params=pltpu.CompilerParams(
            collective_id=0, has_side_effects=True, vmem_limit_bytes=56 * 1024 * 1024
        ),
        cost_estimate=pl.CostEstimate(
            flops=8 * SPAN * SPAN * width, bytes_accessed=6 * SPAN * width, transcendentals=0
        ),
    )(
        x_in,
        z_in,
        b_in,
        c_in,
        dt_raw.T,
        dt_bias[None, :],
        a_log[None, :],
        d_skip[None, :],
        conv_x,
        conv_b,
        conv_c,
    )
    share = rows // 2 if rows % 256 == 0 else rows
    return pl.pallas_call(
        functools.partial(normalise, rows),
        grid=(rows // share,),
        out_shape=jax.ShapeDtypeStruct((rows, n * SPAN), bf16),
        in_specs=[
            pl.BlockSpec((n, share, SPAN), lambda i: (0, i, 0)),
            pl.BlockSpec((n, 8, LANES), lambda i: (0, 0, 0)),
            pl.BlockSpec(gain.shape, lambda i: (0, 0)),
        ],
        out_specs=pl.BlockSpec((share, n * SPAN), lambda i: (i, 0)),
        scratch_shapes=[pltpu.VMEM((rows, LANES), f32)],
        compiler_params=pltpu.CompilerParams(vmem_limit_bytes=56 * 1024 * 1024),
    )(gated, scales, gain)


def solution(mesh):
    return jax.shard_map(
        shards,
        mesh=mesh,
        in_specs=(
            P("ctx", "tp"),
            P("ctx", "tp"),
            P("ctx", "tp"),
            P("ctx", "tp"),
            P("ctx", "tp"),
            P("tp"),
            P("tp"),
            P("tp"),
            P(None, "tp"),
            P(None, "tp"),
            P(None, "tp"),
            P("tp"),
        ),
        out_specs=P(("tp", "ctx"), None),
        check_vma=False,
    )
```

```python
import functools

import jax
import jax.numpy as jnp
from jax import lax
from jax.experimental import pallas as pl
from jax.experimental.pallas import tpu as pltpu
from jax.sharding import PartitionSpec as P

SPAN = 128
LANES = 128
HALO = 16
CHUNKS = 8
EPS = 1e-05
LOG2E = 1.4426950408889634
MESH = pl.DeviceIdType.MESH


def silu(value):
    half = 0.5 * value
    return half + half * jnp.tanh(half)


def conv_silu(pad, taps, count):
    total = taps[0:1] * pad[8 - count + 1 : 8 - count + 1 + SPAN, :]
    for tap in range(1, count):
        start = 8 - count + 1 + tap
        total = total + taps[tap : tap + 1] * pad[start : start + SPAN, :]
    return silu(total).astype(jnp.bfloat16)


def kernel(
    n,
    x_ref,
    z_ref,
    b_ref,
    c_ref,
    dt_ref,
    bias_ref,
    alog_ref,
    skip_ref,
    cx_ref,
    cb_ref,
    cc_ref,
    recv,
    scale_in,
    x_buf,
    z_buf,
    b_buf,
    c_buf,
    cx_buf,
    cb_buf,
    cc_buf,
    halo_x,
    halo_b,
    halo_c,
    small,
    pad,
    x_t,
    z_t,
    pre,
    upd,
    state_in,
    state_out,
    stage,
    scale_out,
    log_rows,
    mix_rows,
    grow_rows,
    last_rows,
    skip_rows,
    cols,
    turned_cols,
    scores,
    b_act,
    c_act,
    ssq,
    above,
    load,
    halo_send,
    halo_recv,
    state_send,
    state_recv,
    out_send,
    out_recv,
    scale_send,
    scale_recv,
):
    width = x_ref.shape[1]
    heads = dt_ref.shape[0]
    head = width // heads
    per_block = LANES // head
    chunk = width // CHUNKS
    blocks = chunk // LANES
    chunk_heads = heads // CHUNKS
    rows = width // n
    parts = chunk // rows
    taps = cx_ref.shape[0]
    me = lax.axis_index("ctx")
    nxt = lax.rem(me + 1, n)

    barrier = pltpu.get_barrier_semaphore()

    def greet(other):
        pl.semaphore_signal(barrier, inc=1, device_id={"ctx": other}, device_id_type=MESH)

    @pl.when(me > 0)
    def _():
        greet(me - 1)

    @pl.when(me < n - 1)
    def _():
        greet(me + 1)

    def tell_above():
        pl.semaphore_signal(above, inc=1, device_id={"ctx": me - 1}, device_id_type=MESH)

    def pass_above():
        pl.semaphore_wait(above, 1)

        @pl.when(me > 0)
        def _():
            tell_above()

    def halo_copy(index):
        source = (b_ref, c_ref)[index]
        target = (halo_b, halo_c)[index]
        return pltpu.make_async_remote_copy(
            src_ref=source.at[pl.ds(SPAN - HALO, HALO), :],
            dst_ref=target,
            send_sem=halo_send.at[CHUNKS + index],
            recv_sem=halo_recv.at[CHUNKS + index],
            device_id={"ctx": nxt},
            device_id_type=MESH,
        )

    def halo_x_copy(k):
        place = pl.ds(pl.multiple_of(k * chunk, LANES), chunk)
        return pltpu.make_async_remote_copy(
            src_ref=x_ref.at[pl.ds(SPAN - HALO, HALO), place],
            dst_ref=halo_x.at[:, place],
            send_sem=halo_send.at[k],
            recv_sem=halo_recv.at[k],
            device_id={"ctx": nxt},
            device_id_type=MESH,
        )

    pieces = min(4, blocks)
    piece = chunk // pieces

    def state_copy(k, p):
        return pltpu.make_async_remote_copy(
            src_ref=state_out.at[k, pl.ds(p * piece, piece), :],
            dst_ref=state_in.at[k, pl.ds(p * piece, piece), :],
            send_sem=state_send.at[k, p],
            recv_sem=state_recv.at[k, p],
            device_id={"ctx": nxt},
            device_id_type=MESH,
        )

    def out_copy(k, part, dest, slot):
        return pltpu.make_async_remote_copy(
            src_ref=stage.at[k, pl.ds(part * rows, rows), :],
            dst_ref=recv.at[slot],
            send_sem=out_send.at[dest],
            recv_sem=out_recv.at[slot],
            device_id={"ctx": dest},
            device_id_type=MESH,
        )

    def own_out(k, part):
        return pltpu.make_async_copy(
            stage.at[k, pl.ds(part * rows, rows), :], recv.at[me], out_recv.at[me]
        )

    def own_scale():
        return pltpu.make_async_copy(scale_out, scale_in.at[me], scale_recv.at[me])

    def scale_copy(dest, slot):
        return pltpu.make_async_remote_copy(
            src_ref=scale_out,
            dst_ref=scale_in.at[slot],
            send_sem=scale_send.at[dest],
            recv_sem=scale_recv.at[slot],
            device_id={"ctx": dest},
            device_id_type=MESH,
        )

    def loading(index):
        source = (x_ref, b_ref, c_ref, cx_ref, cb_ref, cc_ref, z_ref)[index]
        target = (x_buf, b_buf, c_buf, cx_buf, cb_buf, cc_buf, z_buf)[index]
        return pltpu.make_async_copy(source, target, load.at[index])

    for index in range(7):
        loading(index).start()

    def down_columns(row, count):
        return jnp.broadcast_to(row, (SPAN, count)).T

    small[...] = jnp.zeros_like(small)
    small[SPAN : SPAN + 1, 0:heads] = bias_ref[...]
    small[SPAN + 8 : SPAN + 9, 0:heads] = alog_ref[...]
    small[SPAN + 16 : SPAN + 17, 0:heads] = skip_ref[...]
    small[0:heads, :] = dt_ref[...]
    raw = small[0:SPAN, :] + down_columns(small[SPAN : SPAN + 1, :], LANES)
    delta = jnp.maximum(raw, 0.0) + jnp.log1p(jnp.exp(-jnp.abs(raw)))
    rate = -down_columns(jnp.exp(small[SPAN + 8 : SPAN + 9, :]), LANES) * delta
    down = lax.broadcasted_iota(jnp.int32, (SPAN, SPAN), 0)
    across = lax.broadcasted_iota(jnp.int32, (SPAN, SPAN), 1)
    upper = jnp.where(down <= across, 1.0, 0.0)
    logs = jnp.dot(
        rate, upper, precision=lax.Precision.HIGHEST, preferred_element_type=jnp.float32
    )
    last = jnp.broadcast_to(logs[:, SPAN - 1 : SPAN], (SPAN, LANES))
    log_rows[...] = logs * LOG2E
    mix_rows[...] = jnp.exp(last - logs) * delta
    last_rows[...] = jnp.exp(last)
    turned_cols[...] = (logs - jnp.log(delta)) * LOG2E

    ends = (me == 0) | (me == n - 1)

    @pl.when(ends)
    def _():
        pl.semaphore_wait(barrier, 1)

    @pl.when(jnp.logical_not(ends))
    def _():
        pl.semaphore_wait(barrier, 2)

    @pl.when(me == n - 1)
    def _():
        tell_above()

    @pl.when(me < n - 1)
    def _():
        halo_copy(0).start()
        halo_x_copy(0).start()
        halo_copy(1).start()
        for k in range(1, CHUNKS):
            halo_x_copy(k).start()

    early = me < n // 2

    @pl.when(jnp.logical_not(early) & (me < n - 1))
    def _():
        pass_above()

    for index in range(6):
        loading(index).wait()

    @pl.when(me > 0)
    def _():
        halo_copy(0).wait_recv()

    @pl.when(me == 0)
    def _():
        halo_x[...] = jnp.zeros_like(halo_x)
        halo_b[...] = jnp.zeros_like(halo_b)
        halo_c[...] = jnp.zeros_like(halo_c)
        state_in[...] = jnp.zeros_like(state_in)

    def project(slot, source, halo, weights, target):
        pad[slot, 0:8, :] = halo[...].astype(jnp.float32)[HALO - 8 :]
        pad[slot, 8 : 8 + SPAN, :] = source[...].astype(jnp.float32)
        target[...] = conv_silu(pad.at[slot], weights[...], taps)

    project(0, b_buf, halo_b, cb_buf, b_act)

    def head_row(ref, index):
        return jnp.broadcast_to(ref[pl.ds(index, 1), :], (head, LANES))

    def block_rows(ref, k, j):
        first = k * chunk_heads + j * per_block
        return jnp.concatenate([head_row(ref, first + i) for i in range(per_block)], axis=0)

    def block_place(k, j):
        return pl.ds(pl.multiple_of(k * chunk + j * LANES, LANES), LANES)

    def chain(k):
        for p in range(pieces):

            @pl.when(me > 0)
            def _():
                state_copy(k, p).wait_recv()

            @pl.when(me < n - 1)
            def _():
                for j in range(p * piece // LANES, (p + 1) * piece // LANES):
                    entering = state_in[k, j * LANES : (j + 1) * LANES, :].astype(jnp.float32)
                    leaving = block_rows(last_rows, k, j) * entering + upd[block_place(k, j), :]
                    state_out[k, j * LANES : (j + 1) * LANES, :] = leaving.astype(jnp.bfloat16)
                state_copy(k, p).start()

    def set_up():
        @pl.when(me > 0)
        def _():
            halo_copy(1).wait_recv()

        project(1, c_buf, halo_c, cc_buf, c_act)
        overlap = lax.dot_general(
            b_act[...], c_act[...], (((1,), (1,)), ((), ())), preferred_element_type=jnp.float32
        )
        scores[...] = jnp.where(down <= across, overlap, 0.0)
        grow_rows[...] = jnp.exp2(log_rows[...])
        skip_rows[...] = down_columns(small[SPAN + 16 : SPAN + 17, :], LANES)
        shifted = turned_cols[...].T
        for k in range(CHUNKS):
            cols[k, :, 0:chunk_heads] = shifted[:, k * chunk_heads : (k + 1) * chunk_heads]
        ssq[...] = jnp.zeros_like(ssq)

    def within(k):
        shifts = cols[k]
        for j in range(blocks):
            place = block_place(k, j)
            z_t[place, :] = silu(z_buf[:, place].T.astype(jnp.float32))
            x_block = x_t[place, :]
            inner = []
            for i in range(per_block):
                which = j * per_block + i
                gap = (
                    log_rows[pl.ds(k * chunk_heads + which, 1), :] - shifts[:, which : which + 1]
                )
                weights = (scores[...] * jnp.exp2(gap)).astype(jnp.bfloat16)
                inner.append(
                    jnp.dot(
                        x_block[i * head : (i + 1) * head],
                        weights,
                        preferred_element_type=jnp.float32,
                    )
                )
            pre[place, :] = jnp.concatenate(inner, axis=0) + block_rows(
                skip_rows, k, j
            ) * x_block.astype(jnp.float32)

    middle = early & (me > 0)
    lag = jnp.where(middle, jnp.minimum(2 * (me - 1), CHUNKS), 0)

    far_first = me == n // 2 - 1

    def order(step):
        return jnp.where(far_first, lax.rem(step + CHUNKS // 2, CHUNKS), step)

    def updates(k):
        @pl.when(me > 0)
        def _():
            halo_x_copy(k).wait_recv()

        for j in range(blocks):
            place = block_place(k, j)
            pad[j, 0:8, :] = halo_x[:, place].astype(jnp.float32)[HALO - 8 :]
            pad[j, 8 : 8 + SPAN, :] = x_buf[:, place].astype(jnp.float32)
            act = conv_silu(pad.at[j], cx_buf[:, place], taps)
            turned = act.T
            x_t[place, :] = turned
            scaled = (turned.astype(jnp.float32) * block_rows(mix_rows, k, j)).astype(jnp.bfloat16)
            upd[place, :] = jnp.dot(scaled, b_act[...], preferred_element_type=jnp.float32)

    def advance(step, carry):
        @pl.when(step < CHUNKS)
        def _():
            updates(step)

        @pl.when(step >= CHUNKS)
        def _():
            within(order(step - CHUNKS))

        turn = lag + jnp.minimum(2 * (n // 2 - 1 - me) + 1, CHUNKS - 1)

        @pl.when(middle & (step == turn))
        def _():
            pass_above()

        @pl.when(early & (step >= lag))
        def _():
            chain(step - lag)

        return carry

    @pl.when(me > 1)
    def _():
        set_up()

    loading(6).wait()
    lax.fori_loop(0, CHUNKS + lag, advance, 0)

    @pl.when(me <= 1)
    def _():
        set_up()

    ahead = jnp.where(early, lag, jnp.minimum(2 * (me - n // 2) + 2, CHUNKS))
    ahead = jnp.where(me == 0, CHUNKS // 2, ahead)

    def within_ahead(k, carry):
        within(k)
        return carry

    lax.fori_loop(lag, ahead, within_ahead, 0)

    @pl.when(me == 0)
    def _():
        pass_above()

    def outputs(step, carry):
        k = order(step)

        @pl.when(step >= ahead)
        def _():
            within(k)

        @pl.when(jnp.logical_not(early))
        def _():
            chain(k)

        squares = ssq[0:1, :]
        for j in range(blocks):
            place = block_place(k, j)
            outer = lax.dot_general(
                state_in[k, j * LANES : (j + 1) * LANES, :],
                c_act[...],
                (((1,), (1,)), ((), ())),
                preferred_element_type=jnp.float32,
            )
            gated = (pre[place, :] + block_rows(grow_rows, k, j) * outer) * z_t[place, :]
            squares = squares + jnp.sum(gated * gated, axis=0, keepdims=True)
            stage[k, j * LANES : (j + 1) * LANES, :] = gated.astype(jnp.bfloat16)
        ssq[0:1, :] = squares

        for part in range(parts):
            dest = k * parts + part

            @pl.when(dest != me)
            def _():
                out_copy(k, part, dest, me).start()

            @pl.when(dest == me)
            def _():
                own_out(k, part).start()

        return carry

    lax.fori_loop(0, CHUNKS, outputs, 0)

    scale = jnp.broadcast_to(lax.rsqrt(ssq[0:1, :] / width + EPS), (8, LANES))
    scale_out[...] = scale
    own_scale().start()

    def tell(other, carry):
        @pl.when(other != me)
        def _():
            scale_copy(other, me).start()

        return carry

    lax.fori_loop(0, n, tell, 0)

    def finish(source, carry):
        @pl.when(source != me)
        def _():
            out_copy(0, 0, source, source).wait_recv()
            scale_copy(source, source).wait_recv()

        @pl.when(source == me)
        def _():
            own_out(0, 0).wait()
            own_scale().wait()

        return carry

    lax.fori_loop(0, n, finish, 0)

    @pl.when(me < n - 1)
    def _():
        for index in range(2):
            halo_copy(index).wait_send()

        def drain_state(k, carry):
            halo_x_copy(k).wait_send()
            for p in range(pieces):
                state_copy(k, p).wait_send()
            return carry

        lax.fori_loop(0, CHUNKS, drain_state, 0)

    def drain(other, carry):
        @pl.when(other != me)
        def _():
            out_copy(0, 0, other, me).wait_send()
            scale_copy(other, me).wait_send()

        return carry

    lax.fori_loop(0, n, drain, 0)


def normalise(rows, gated_ref, scale_ref, gain_ref, out_ref, gain_col):
    me = lax.axis_index("ctx")
    step = pl.program_id(0)
    share = out_ref.shape[0]

    @pl.when(step == 0)
    def _():
        if rows % LANES == 0:
            own = gain_ref[:, pl.ds(pl.multiple_of(me * rows, LANES), rows)]
        else:
            own = gain_ref[pl.ds(me, 1), :]
        gain_col[...] = jnp.broadcast_to(own, (LANES, rows)).T

    gain = gain_col[pl.ds(pl.multiple_of(step * share, share), share), :]
    for i in range(gated_ref.shape[0]):
        value = gated_ref[i].astype(jnp.float32) * scale_ref[i, 0:1, :] * gain
        out_ref[:, i * SPAN : (i + 1) * SPAN] = value.astype(jnp.bfloat16)


def shards(
    x_in, z_in, b_in, c_in, dt_raw, dt_bias, a_log, d_skip, conv_x, conv_b, conv_c, norm_gain
):
    n = lax.axis_size("ctx")
    width = x_in.shape[1]
    state = b_in.shape[1]
    rows = width // n
    chunk = width // CHUNKS
    gain = norm_gain.reshape((1, width) if rows % LANES == 0 else (n, rows))
    taps = conv_x.shape[0]
    hbm = pl.BlockSpec(memory_space=pl.ANY)
    vmem = pl.BlockSpec(memory_space=pltpu.VMEM)
    f32, bf16 = jnp.float32, jnp.bfloat16
    dma = pltpu.SemaphoreType.DMA
    square = pltpu.VMEM((LANES, LANES), f32)
    gated, scales = pl.pallas_call(
        functools.partial(kernel, n),
        out_shape=(
            jax.ShapeDtypeStruct((n, rows, SPAN), bf16),
            jax.ShapeDtypeStruct((n, 8, LANES), f32),
        ),
        in_specs=[hbm] * 4 + [vmem] * 4 + [hbm] * 3,
        out_specs=(hbm, hbm),
        scratch_shapes=[
            pltpu.VMEM((SPAN, width), bf16),
            pltpu.VMEM((SPAN, width), bf16),
            pltpu.VMEM((SPAN, state), bf16),
            pltpu.VMEM((SPAN, state), bf16),
            pltpu.VMEM((taps, width), f32),
            pltpu.VMEM((taps, state), f32),
            pltpu.VMEM((taps, state), f32),
            pltpu.VMEM((HALO, width), bf16),
            pltpu.VMEM((HALO, state), bf16),
            pltpu.VMEM((HALO, state), bf16),
            pltpu.VMEM((SPAN + 24, LANES), f32),
            pltpu.VMEM((max(2, chunk // LANES), SPAN + 8, LANES), f32),
            pltpu.VMEM((width, SPAN), bf16),
            pltpu.VMEM((width, SPAN), f32),
            pltpu.VMEM((width, SPAN), f32),
            pltpu.VMEM((width, state), f32),
            pltpu.VMEM((CHUNKS, chunk, state), bf16),
            pltpu.VMEM((CHUNKS, chunk, state), bf16),
            pltpu.VMEM((CHUNKS, chunk, SPAN), bf16),
            pltpu.VMEM((8, LANES), f32),
            square,
            square,
            square,
            square,
            square,
            pltpu.VMEM((CHUNKS, SPAN, LANES), f32),
            square,
            square,
            pltpu.VMEM((SPAN, state), bf16),
            pltpu.VMEM((SPAN, state), bf16),
            pltpu.VMEM((8, LANES), f32),
            pltpu.SemaphoreType.REGULAR,
            dma((7,)),
            dma((CHUNKS + 2,)),
            dma((CHUNKS + 2,)),
            dma((CHUNKS, 4)),
            dma((CHUNKS, 4)),
            dma((n,)),
            dma((n,)),
            dma((n,)),
            dma((n,)),
        ],
        compiler_params=pltpu.CompilerParams(
            collective_id=0, has_side_effects=True, vmem_limit_bytes=56 * 1024 * 1024
        ),
        cost_estimate=pl.CostEstimate(
            flops=8 * SPAN * SPAN * width, bytes_accessed=6 * SPAN * width, transcendentals=0
        ),
    )(
        x_in,
        z_in,
        b_in,
        c_in,
        dt_raw.T,
        dt_bias[None, :],
        a_log[None, :],
        d_skip[None, :],
        conv_x,
        conv_b,
        conv_c,
    )
    share = rows // 2 if rows % 256 == 0 else rows
    return pl.pallas_call(
        functools.partial(normalise, rows),
        grid=(rows // share,),
        out_shape=jax.ShapeDtypeStruct((rows, n * SPAN), bf16),
        in_specs=[
            pl.BlockSpec((n, share, SPAN), lambda i: (0, i, 0)),
            pl.BlockSpec((n, 8, LANES), lambda i: (0, 0, 0)),
            pl.BlockSpec(gain.shape, lambda i: (0, 0)),
        ],
        out_specs=pl.BlockSpec((share, n * SPAN), lambda i: (i, 0)),
        scratch_shapes=[pltpu.VMEM((rows, LANES), f32)],
        compiler_params=pltpu.CompilerParams(vmem_limit_bytes=56 * 1024 * 1024),
    )(gated, scales, gain)


def solution(mesh):
    return jax.shard_map(
        shards,
        mesh=mesh,
        in_specs=(
            P("ctx", "tp"),
            P("ctx", "tp"),
            P("ctx", "tp"),
            P("ctx", "tp"),
            P("ctx", "tp"),
            P("tp"),
            P("tp"),
            P("tp"),
            P(None, "tp"),
            P(None, "tp"),
            P(None, "tp"),
            P("tp"),
        ),
        out_specs=P(("tp", "ctx"), None),
        check_vma=False,
    )
```
